32 devices in a mesh: group: 4 (over x, core), tp: 8 (over z, y).
Axes of the slice: x: 2, y: 2, z: 4, core: 2. Of those that a mesh axis runs over, the one named last changes fastest.
Arguments:
- prefill_x: bfloat16 [512, 16384], P('group', 'tp'), may hold values from -6 to 6
- prefill_gate: bfloat16 [512, 16384], P('group', 'tp'), may hold values from -6 to 6
- lengths: int32 [4, 8], P('group'), may hold values from 1 to 64, 128 in all within a row
- routes: int32 [32, 1], replicated, may hold values from 0 to 3; in each aligned block of 8 rows (0 to 7, 8 to 15, ...) at most 4 rows name the same one
- decode_x: bfloat16 [4, 128, 16384], P(None, 'group', 'tp'), may hold values from -6 to 6
- decode_gate: bfloat16 [4, 128, 16384], P(None, 'group', 'tp'), may hold values from -6 to 6
- cached_state: float32 [128, 16, 16384], P('group', None, 'tp'), may hold values from -4 to 4
- xproj_weight: bfloat16 [16384, 544], P('tp'), may hold values from -0.046875 to 0.046875
- dt_weight: bfloat16 [512, 16384], P(None, 'tp'), may hold values from -0.25 to 0.25
- dt_bias: float32 [16384], P('tp'), may hold values from -3 to -1
- a_log: float32 [16, 16384], P(None, 'tp'), may hold values from 0 to 2.77
- skip_gain: float32 [16384], P('tp'), may hold values from 0.5 to 1.5
Outputs:
- prefill_out: bfloat16 [512, 16384], P('group', 'tp')
- decode_out: bfloat16 [4, 128, 16384], P(None, 'group', 'tp')
The draws below stay inside these ranges and needn't reach their ends.
Inputs may be any that keep to these rules, and one draw needn't show every extreme that they name: `routes`: in each aligned block of 8 rows (the requests of one group) no decode group is named more than 4 times. `lengths`: each group's row sums to 128; its largest entry is 64.
All inputs are finite; a program needn't handle non-finite values.
Results may differ from the reference program's by a relative error of at most 0.0051.
Values sent between devices are 32-bit elements; how exact they have to be, the bound alone decides.
A program may use at most 128 MiB of HBM per device.

```python
import math
import jax
import jax.numpy as jnp
import numpy as np
from jax import lax

E = 16384
S = 16
DT_RANK = 512
TOK = 128
REQ = 8
ROWS = 32
STEPS = 4
MAXLEN = 64
CAP = 4
N_GROUP = 4


def level_of(key, extent, pieces, smallest, top_value):
    def one(axis_at, parts):
        heights = jax.random.uniform(jax.random.fold_in(jax.random.fold_in(key, 6), axis_at), (parts,), jnp.float32, smallest / len(pieces), top_value / len(pieces))
        return jnp.repeat(jnp.exp(heights), extent[axis_at] // parts).reshape((-1,) + (1,) * (len(extent) - axis_at - 1))

    level = one(*pieces[0])
    for cut in pieces[1:]:
        level = level * one(*cut)
    return level


def length_profile(count, total, bound, lean):
    loads = [(1 << 20) // math.isqrt(rank ** lean) + 1 for rank in range(2, count + 1)]
    spare, given = total - bound - (count - 1), [1] * (count - 1)
    while spare > 0:
        candidates = [i for i in range(count - 1) if given[i] < bound]
        mass, budget = sum([loads[i] for i in candidates]), spare
        for i in candidates:
            more = min(bound - given[i], max(1, budget * loads[i] // mass), spare)
            given[i] = given[i] + more
            spare = spare - more
    return np.array([bound] + given)


def uneven(stream_key, amount, total, most, slope):
    if amount == 2:
        one = jax.random.randint(stream_key, (), max(1, total - most), min(most, total - 1) + 1)
        return jnp.stack([one, total - one])
    sizes = jnp.asarray(length_profile(amount, total, most, slope), jnp.int32)
    couples = (amount - 1) // 2
    donor, sink = sizes[1:1 + 2 * couples:2], sizes[2:2 + 2 * couples:2]
    margin = jnp.minimum(donor - 1, most - sink)
    moved = jax.random.randint(jax.random.fold_in(stream_key, 1), (couples,), 0, 1 << 20) % (margin + 1)
    sizes = sizes.at[1:1 + 2 * couples:2].set(donor - moved).at[2:2 + 2 * couples:2].set(sink + moved)
    return sizes[jax.random.permutation(jax.random.fold_in(stream_key, 2), amount)]


def assign_block(own_key, own, number, rows, count, top, most, lean):
    ranking = jax.random.permutation(own_key, count)
    heavy_load, ordinary = shares(count, rows * top, most, lean, True), shares(count, rows * top, most, lean, False)
    places = jnp.arange(count)

    def named(tallies, rotation):
        used = int((tallies > 0).sum())
        fixed = max(1, used // 4)
        shifted = fixed + (places - fixed + rotation * (used - fixed)) % max(1, count - fixed)
        return jnp.zeros((count,), jnp.int32).at[ranking[jnp.where(places < fixed, places, shifted)]].set(jnp.asarray(tallies, jnp.int32))

    tallies = jnp.where(number % 4 == 0, named(heavy_load, number // 4), named(ordinary, number - number // 4 - 1))
    mixed = jax.random.permutation(jax.random.fold_in(own, 3), count)
    source_of, taker = mixed[0:count // 2 * 2:2], mixed[1:count // 2 * 2:2]
    margin = jnp.minimum(tallies[source_of] - 1, most - tallies[taker]) // 2
    margin = jnp.where((source_of == ranking[0]) | (taker == ranking[0]) | (tallies[taker] == 0), 0, jnp.maximum(margin, 0))
    shifted = jax.random.randint(jax.random.fold_in(own, 4), (count // 2,), 0, 1 << 20) % (margin + 1)
    tallies = tallies.at[source_of].add(-shifted).at[taker].add(shifted)
    members = jnp.searchsorted(jnp.cumsum(tallies), jnp.arange(rows * top), side="right").astype(jnp.int32)
    table = members.reshape(top, rows).T
    table = table[jax.random.permutation(jax.random.fold_in(own, 1), rows)]
    rotation = jax.random.randint(jax.random.fold_in(own, 2), (rows, 1), 0, top)
    return jnp.take_along_axis(table, (jnp.arange(top)[None, :] + rotation) % top, axis=1)


def shares(count, total, most, lean, full):
    weights = [(1 << 20) // math.isqrt(grade ** lean) + 1 for grade in range(1, count + 1)]
    largest = most if full else min(most, max(-(-total // count), total * weights[0] // sum(weights)))
    least = 1 if total - largest >= count - 1 else 0
    counts, spare = [largest] + [least] * (count - 1), total - largest - least * (count - 1)
    while spare > 0:
        free = [i for i in range(1, count) if counts[i] < largest] or [i for i in range(1, count) if counts[i] < most]
        mass, budget = sum([weights[i] for i in free]), spare
        for i in free:
            extra = min(most - counts[i], max(1, budget * weights[i] // mass), spare)
            counts[i] = counts[i] + extra
            spare = spare - extra
    return np.array(counts)


def scatter_about(own_key, extent, spread, reach, pieces=(), held_as=jnp.bfloat16):
    loudness = level_of(own_key, extent, pieces, -0.22, 0.18) if pieces else 1.0
    drawn = jax.random.normal(own_key, extent, jnp.float32) * spread * loudness
    return jnp.minimum(jnp.maximum(drawn, -reach), reach).astype(held_as)


def setup_inputs(seed: int = 0) -> dict:
    seeds = jax.random.split(jax.random.key(seed), 13)
    prefill_x = scatter_about(seeds[0], (N_GROUP * TOK, E), 1.0, 6.0, ((0, 4), (1, 8)))
    prefill_gate = scatter_about(seeds[1], (N_GROUP * TOK, E), 1.0, 6.0, ((0, 4), (1, 8)))
    lengths = jax.vmap(lambda own: uneven(own, REQ, TOK, MAXLEN, 2))(jax.random.split(seeds[2], N_GROUP)).reshape((N_GROUP, REQ)).astype(jnp.int32)
    routes_keys = jax.random.split(jax.random.fold_in(seeds[3], 1), (N_GROUP * REQ) // REQ)
    routes_turns = jax.random.permutation(jax.random.fold_in(seeds[3], 3), (N_GROUP * REQ) // REQ)
    routes = jax.vmap(lambda own, number: assign_block(jax.random.fold_in(seeds[3], 2), own, number, REQ, N_GROUP, 1, CAP, 2))(routes_keys, routes_turns).reshape((N_GROUP * REQ, 1))
    decode_x = scatter_about(seeds[4], (STEPS, N_GROUP * ROWS, E), 1.0, 6.0, ((1, 4), (2, 8)))
    decode_gate = scatter_about(seeds[5], (STEPS, N_GROUP * ROWS, E), 1.0, 6.0, ((1, 4), (2, 8)))
    cached_state = scatter_about(seeds[6], (N_GROUP * ROWS, S, E), 0.5, 4.0, ((0, 4), (2, 8)), jnp.float32)
    xproj_weight = scatter_about(seeds[7], (E, DT_RANK + 2 * S), E ** -0.5, 0.046875, ((0, 8),))
    dt_weight = scatter_about(seeds[8], (DT_RANK, E), DT_RANK ** -0.5, 0.25, ((1, 8),))
    dt_bias = jnp.clip(-3.0 + 2.0 * jax.random.uniform(seeds[9], (E,), jnp.float32) ** level_of(seeds[9], (E,), ((0, 8),), -0.2, 0.2), -3.0, -1.0)
    a_log = jnp.clip(2.77 * jax.random.uniform(seeds[10], (S, E), jnp.float32) ** level_of(seeds[10], (S, E), ((1, 8),), -0.2, 0.2), 0.0, 2.77)
    skip_gain = jnp.clip(0.5 + 1.0 * jax.random.uniform(seeds[11], (E,), jnp.float32) ** level_of(seeds[11], (E,), ((0, 8),), -0.2, 0.2), 0.5, 1.5)
    return dict(prefill_x=prefill_x, prefill_gate=prefill_gate, lengths=lengths, routes=routes, decode_x=decode_x, decode_gate=decode_gate, cached_state=cached_state, xproj_weight=xproj_weight, dt_weight=dt_weight, dt_bias=dt_bias, a_log=a_log, skip_gain=skip_gain)


def mixer_terms(projected, dt_weight, dt_bias):
    low_part = projected[:, :DT_RANK].astype(jnp.bfloat16)
    step_size = jax.nn.softplus(jnp.dot(low_part, dt_weight, preferred_element_type=jnp.float32) + dt_bias)
    return step_size, projected[:, DT_RANK:DT_RANK + S], projected[:, DT_RANK + S:]


def prefill_group(operands, xproj_weight, dt_weight, dt_bias, rates, skip_gain):
    inputs, gate_rows, lengths_here = operands
    projected = jnp.dot(inputs, xproj_weight, preferred_element_type=jnp.float32)
    step_size, inject, readout = mixer_terms(projected, dt_weight, dt_bias)
    request_end = (jnp.cumsum(lengths_here) - 1).astype(jnp.int32)
    request_start = (request_end - lengths_here + 1).astype(jnp.int32)
    position = jnp.arange(TOK, dtype=jnp.int32)
    first_token = jnp.any(position[:, None] == request_start[None, :], axis=1)
    last_token = jnp.any(position[:, None] == request_end[None, :], axis=1)
    request_of = (jnp.sum((position[:, None] >= request_start[None, :]).astype(jnp.int32), axis=1) - 1).astype(jnp.int32)
    survive = jnp.where(first_token, jnp.float32(0.0), jnp.float32(1.0))
    values = inputs.astype(jnp.float32)

    def advance(carried, slices):
        hidden, final_states = carried
        size_row, inject_row, readout_row, value_row, survive_one, last_one, request_one = slices
        hidden = (survive_one * jnp.exp(size_row[None, :] * rates)) * hidden + (size_row[None, :] * inject_row[:, None]) * value_row[None, :]
        mixed = jnp.sum(readout_row[:, None] * hidden, axis=0)
        previous = lax.dynamic_index_in_dim(final_states, request_one, 0, keepdims=False)
        final_states = lax.dynamic_update_index_in_dim(final_states, jnp.where(last_one, hidden, previous), request_one, 0)
        return (hidden, final_states), mixed

    initial = (jnp.zeros((S, E), jnp.float32), jnp.zeros((REQ, S, E), jnp.float32))
    (hidden, final_states), mixed = lax.scan(advance, initial, (step_size, inject, readout, values, survive, last_token, request_of))
    output = ((mixed + skip_gain * values) * jax.nn.silu(gate_rows.astype(jnp.float32))).astype(jnp.bfloat16)
    return output, final_states


def decode_group(operands, xproj_weight, dt_weight, dt_bias, rates, skip_gain):
    hidden, inputs_all, gates_all = operands
    outputs = []
    for step_index in range(STEPS):
        inputs = inputs_all[step_index]
        projected = jnp.dot(inputs, xproj_weight, preferred_element_type=jnp.float32)
        step_size, inject, readout = mixer_terms(projected, dt_weight, dt_bias)
        values = inputs.astype(jnp.float32)
        hidden = jnp.exp(step_size[:, None, :] * rates[None]) * hidden + (step_size[:, None, :] * inject[:, :, None]) * values[:, None, :]
        mixed = jnp.sum(readout[:, :, None] * hidden, axis=1)
        gate_rows = gates_all[step_index].astype(jnp.float32)
        outputs.append(((mixed + skip_gain * values) * jax.nn.silu(gate_rows)).astype(jnp.bfloat16))
    return jnp.stack(outputs)


def reference(prefill_x, prefill_gate, lengths, routes, decode_x, decode_gate, cached_state, xproj_weight, dt_weight, dt_bias, a_log, skip_gain):
    rates = -jnp.exp(a_log)
    prefill_out, final_states = lax.map(
        lambda operands: prefill_group(operands, xproj_weight, dt_weight, dt_bias, rates, skip_gain),
        (prefill_x.reshape(N_GROUP, TOK, E), prefill_gate.reshape(N_GROUP, TOK, E), lengths))
    prefill_out = prefill_out.reshape(N_GROUP * TOK, E)
    final_states = final_states.reshape(N_GROUP * REQ, S, E)
    flat_routes = routes[:, 0]
    ordering = jnp.arange(N_GROUP * REQ, dtype=jnp.int32)
    same_dest = flat_routes[:, None] == flat_routes[None, :]
    slot_index = jnp.sum(((ordering[:, None] > ordering[None, :]) & same_dest).astype(jnp.int32), axis=1).astype(jnp.int32)
    targets = (flat_routes * ROWS + slot_index).astype(jnp.int32)
    row_ids = jnp.arange(N_GROUP * ROWS, dtype=jnp.int32)
    matches = row_ids[:, None] == targets[None, :]
    arrived = jnp.any(matches, axis=1)
    source = jnp.argmax(matches.astype(jnp.int32), axis=1).astype(jnp.int32)
    start_state = jnp.where(arrived[:, None, None], final_states[source], cached_state)
    decode_out = lax.map(
        lambda operands: decode_group(operands, xproj_weight, dt_weight, dt_bias, rates, skip_gain),
        (start_state.reshape(N_GROUP, ROWS, S, E),
         decode_x.reshape(STEPS, N_GROUP, ROWS, E).transpose(1, 0, 2, 3),
         decode_gate.reshape(STEPS, N_GROUP, ROWS, E).transpose(1, 0, 2, 3)))
    decode_out = decode_out.transpose(1, 0, 2, 3).reshape(STEPS, N_GROUP * ROWS, E)
    return prefill_out, decode_out
```

```python
import functools
import jax
import jax.numpy as jnp
from jax import lax
from jax.experimental import pallas as pl
from jax.experimental.pallas import tpu as pltpu
from jax.sharding import PartitionSpec as P

MESH = pl.DeviceIdType.MESH
F32 = jnp.float32
LOG2E = 1.4426950408889634


def softplus(v):
    return jnp.maximum(v, 0.0) + jnp.log1p(jnp.exp(-jnp.abs(v)))


def silu(v):
    return v / (1.0 + jnp.exp(-v))


def project_kernel(n, px_ref, dx_ref, w_ref, out_ref, part, recv, send_sem, recv_sem, gsend_sem, grecv_sem):
    me = lax.axis_index("tp")
    rows = part.shape[2]
    barrier = pltpu.get_barrier_semaphore()
    for k in range(1, n):
        pl.semaphore_signal(barrier, inc=1, device_id={"tp": lax.rem(me + k, n)}, device_id_type=MESH)

    def scatter(phase, k):
        peer = lax.rem(me + k, n)
        return pltpu.make_async_remote_copy(
            src_ref=part.at[phase, peer],
            dst_ref=recv.at[phase, k - 1],
            send_sem=send_sem.at[phase, k - 1],
            recv_sem=recv_sem.at[phase, k - 1],
            device_id={"tp": peer},
            device_id_type=MESH,
        )

    def gather(phase, k):
        return pltpu.make_async_remote_copy(
            src_ref=out_ref.at[phase, me],
            dst_ref=out_ref.at[phase, me],
            send_sem=gsend_sem.at[phase, k - 1],
            recv_sem=grecv_sem.at[phase, k - 1],
            device_id={"tp": lax.rem(me + k, n)},
            device_id_type=MESH,
        )

    for phase, x_ref in enumerate((px_ref, dx_ref)):
        res = jnp.dot(x_ref[...], w_ref[...], preferred_element_type=F32)
        for j in range(n):
            part[phase, j] = res[j * rows:(j + 1) * rows]
        if phase == 0:
            pl.semaphore_wait(barrier, n - 1)
        for k in range(1, n):
            scatter(phase, k).start()
    for phase in range(2):
        total = part[phase, me]
        for k in range(1, n):
            scatter(phase, k).wait_recv()
            total = total + recv[phase, k - 1]
        out_ref[phase, me] = total
        for k in range(1, n):
            gather(phase, k).start()
    for phase in range(2):
        for k in range(1, n):
            scatter(phase, k).wait_send()
            gather(phase, k).wait_send()
            source = lax.rem(me + n - k, n)
            pltpu.make_async_remote_copy(
                src_ref=out_ref.at[phase, source],
                dst_ref=out_ref.at[phase, source],
                send_sem=gsend_sem.at[phase, k - 1],
                recv_sem=grecv_sem.at[phase, k - 1],
                device_id={"tp": lax.rem(me + k, n)},
                device_id_type=MESH,
            ).wait_recv()


def project(px, dx, w, n):
    tokens, channels = px.shape
    width = w.shape[1]
    rows = tokens // n
    vmem = pl.BlockSpec(memory_space=pltpu.VMEM)
    out = pl.pallas_call(
        functools.partial(project_kernel, n),
        out_shape=jax.ShapeDtypeStruct((2, n, rows, width), F32),
        in_specs=[vmem] * 3,
        out_specs=vmem,
        scratch_shapes=[
            pltpu.VMEM((2, n, rows, width), F32),
            pltpu.VMEM((2, n - 1, rows, width), F32),
            pltpu.SemaphoreType.DMA((2, n - 1)),
            pltpu.SemaphoreType.DMA((2, n - 1)),
            pltpu.SemaphoreType.DMA((2, n - 1)),
            pltpu.SemaphoreType.DMA((2, n - 1)),
        ],
        compiler_params=pltpu.CompilerParams(
            collective_id=0, has_side_effects=True, vmem_limit_bytes=40 * 1024 * 1024
        ),
        name="project",
    )(px, dx, w)
    return out.reshape(2, tokens, width)


def step_sizes(proj, rank, w_ref, bias_ref):
    low = proj[:, :rank].astype(jnp.bfloat16)
    return softplus(jnp.dot(low, w_ref[...], preferred_element_type=F32) + bias_ref[...])


def prefill_kernel(proj_ref, x_ref, gate_ref, len_ref, w_ref, bias_ref, alog_ref, skip_ref,
                   out_ref, fin_ref, decay, force, mix, hs):
    rank = w_ref.shape[0]
    tokens, block = x_ref.shape
    states = alog_ref.shape[0]
    requests = fin_ref.shape[0]
    step = step_sizes(proj_ref[0], rank, w_ref, bias_ref)
    position = lax.broadcasted_iota(jnp.int32, (tokens, block), 0)
    first = position == 0
    ends = []
    at = jnp.int32(0)
    for k in range(requests):
        at = at + len_ref[0, k]
        ends.append(at - 1)
        if k < requests - 1:
            first = first | (position == at)
    values = x_ref[...].astype(F32)
    decay[...] = jnp.where(first, 1e30, step)
    force[...] = step * values
    rates = -jnp.exp(alog_ref[...]) * LOG2E

    def body(b, h):
        base = pl.multiple_of(b * 8, 8)
        d8 = decay[pl.ds(base, 8), :]
        f8 = force[pl.ds(base, 8), :]
        bc = proj_ref[0, pl.ds(base, 8), rank:rank + 2 * states].T
        rows = []
        for j in range(8):
            da = jnp.exp2(d8[j:j + 1] * rates)
            h = da * h + bc[:states, j:j + 1] * f8[j:j + 1]
            hs[base + j] = h
            rows.append(jnp.sum(bc[states:, j:j + 1] * h, axis=0, keepdims=True))
        mix[pl.ds(base, 8), :] = jnp.concatenate(rows, axis=0)
        return h

    lax.fori_loop(0, tokens // 8, body, jnp.zeros((states, block), F32))
    for k in range(requests):
        fin_ref[k] = hs[ends[k]]
    out_ref[...] = ((mix[...] + skip_ref[...] * values) * silu(gate_ref[...].astype(F32))).astype(out_ref.dtype)


def prefill(proj, x, gate, lengths, w, bias, alog, skip, block):
    tokens, channels = x.shape
    rank, states = w.shape[0], alog.shape[0]
    requests = lengths.shape[1]
    lane = lambda rows: pl.BlockSpec((rows, block), lambda i: (0, i))
    return pl.pallas_call(
        prefill_kernel,
        grid=(channels // block,),
        out_shape=(
            jax.ShapeDtypeStruct((tokens, channels), jnp.bfloat16),
            jax.ShapeDtypeStruct((requests, states, channels), F32),
        ),
        in_specs=[
            pl.BlockSpec((1,) + proj.shape[1:], lambda i: (0, 0, 0)),
            lane(tokens), lane(tokens),
            pl.BlockSpec(memory_space=pltpu.SMEM),
            lane(rank), lane(1), lane(states), lane(1),
        ],
        out_specs=(lane(tokens), pl.BlockSpec((requests, states, block), lambda i: (0, 0, i))),
        scratch_shapes=[
            pltpu.VMEM((tokens, block), F32),
            pltpu.VMEM((tokens, block), F32),
            pltpu.VMEM((tokens, block), F32),
            pltpu.VMEM((tokens, states, block), F32),
        ],
        compiler_params=pltpu.CompilerParams(vmem_limit_bytes=40 * 1024 * 1024),
        name="prefill",
    )(proj, x, gate, lengths, w, bias, alog, skip)


def decode_kernel(proj_ref, x_ref, gate_ref, cache_ref, pool_ref, routes_ref, w_ref, bias_ref, alog_ref, skip_ref,
                  out_ref, decay, force, mix, source):
    rank = w_ref.shape[0]
    steps, rows, block = x_ref.shape
    states = alog_ref.shape[0]
    mine = lax.axis_index("group")
    for i in range(rows):
        source[i] = 0

    def find(r, count):
        hit = routes_ref[r, 0] == mine

        @pl.when(hit)
        def _():
            source[count] = r

        return count + hit.astype(jnp.int32)

    count = lax.fori_loop(0, routes_ref.shape[0], find, jnp.int32(0))
    step = step_sizes(proj_ref[0], rank, w_ref, bias_ref)
    values = x_ref[...].astype(F32)
    decay[...] = step.reshape(steps, rows, block)
    force[...] = decay[...] * values
    rates = -jnp.exp(alog_ref[...]) * LOG2E

    def body(b, carry):
        base = pl.multiple_of(b * 8, 8)
        bcs = [proj_ref[0, pl.ds(pl.multiple_of(i * rows + base, 8), 8), rank:rank + 2 * states].T for i in range(steps)]
        outs = [[] for _ in range(steps)]
        d8 = [decay[i, pl.ds(base, 8), :] for i in range(steps)]
        f8 = [force[i, pl.ds(base, 8), :] for i in range(steps)]
        for j in range(8):
            n = base + j
            h = jnp.where(n < count, pool_ref[source[n]], cache_ref[n])
            for i in range(steps):
                da = jnp.exp2(d8[i][j:j + 1] * rates)
                h = da * h + bcs[i][:states, j:j + 1] * f8[i][j:j + 1]
                outs[i].append(jnp.sum(bcs[i][states:, j:j + 1] * h, axis=0, keepdims=True))
        for i in range(steps):
            mix[i, pl.ds(base, 8), :] = jnp.concatenate(outs[i], axis=0)
        return carry

    lax.fori_loop(0, rows // 8, body, 0)
    out_ref[...] = ((mix[...] + skip_ref[...] * values) * silu(gate_ref[...].astype(F32))).astype(out_ref.dtype)


def decode(proj, x, gate, cache, pool, routes, w, bias, alog, skip, block):
    steps, rows, channels = x.shape
    rank, states = w.shape[0], alog.shape[0]
    lane = lambda r: pl.BlockSpec((r, block), lambda i: (0, i))
    lane3 = lambda a, r: pl.BlockSpec((a, r, block), lambda i: (0, 0, i))
    return pl.pallas_call(
        decode_kernel,
        grid=(channels // block,),
        out_shape=jax.ShapeDtypeStruct((steps, rows, channels), jnp.bfloat16),
        in_specs=[
            pl.BlockSpec((1,) + proj.shape[1:], lambda i: (1, 0, 0)),
            lane3(steps, rows), lane3(steps, rows), lane3(rows, states), lane3(pool.shape[0], states),
            pl.BlockSpec(memory_space=pltpu.SMEM),
            lane(rank), lane(1), lane(states), lane(1),
        ],
        out_specs=lane3(steps, rows),
        scratch_shapes=[
            pltpu.VMEM((steps, rows, block), F32),
            pltpu.VMEM((steps, rows, block), F32),
            pltpu.VMEM((steps, rows, block), F32),
            pltpu.SMEM((rows,), jnp.int32),
        ],
        compiler_params=pltpu.CompilerParams(vmem_limit_bytes=40 * 1024 * 1024),
        name="decode",
    )(proj, x, gate, cache, pool, routes, w, bias, alog, skip)


def local(n_tp, prefill_x, prefill_gate, lengths, routes, decode_x, decode_gate, cached_state,
          xproj_weight, dt_weight, dt_bias, a_log, skip_gain):
    steps, rows, channels = decode_x.shape
    proj = project(prefill_x, decode_x.reshape(steps * rows, channels), xproj_weight, n_tp)
    bias, skip = dt_bias[None], skip_gain[None]
    out, final = prefill(proj, prefill_x, prefill_gate, lengths, dt_weight, bias, a_log, skip, min(512, channels))
    pool = lax.all_gather(final, "group", axis=0, tiled=True)
    dec = decode(proj, decode_x, decode_gate, cached_state, pool, routes, dt_weight, bias, a_log, skip, min(512, channels))
    return out, dec


def solution(mesh):
    placed = (
        P("group", "tp"),
        P("group", "tp"),
        P("group", None),
        P(),
        P(None, "group", "tp"),
        P(None, "group", "tp"),
        P("group", None, "tp"),
        P("tp", None),
        P(None, "tp"),
        P("tp"),
        P(None, "tp"),
        P("tp"),
    )
    return jax.shard_map(
        functools.partial(local, mesh.shape["tp"]),
        mesh=mesh,
        in_specs=placed,
        out_specs=(P("group", "tp"), P(None, "group", "tp")),
        check_vma=False,
    )
```

```python
import functools
import jax
import jax.numpy as jnp
from jax import lax
from jax.experimental import pallas as pl
from jax.experimental.pallas import tpu as pltpu
from jax.sharding import PartitionSpec as P

MESH = pl.DeviceIdType.MESH
F32 = jnp.float32
BF16 = jnp.bfloat16
LOG2E = 1.4426950408889634
SET = 16


def softplus(v):
    return jnp.maximum(v, 0.0) + jnp.log1p(jnp.exp(-jnp.abs(v)))


def silu(v):
    return v / (1.0 + jnp.exp(-v))


def dot_nt(a, b):
    return lax.dot_general(a, b, (((1,), (1,)), ((), ())), preferred_element_type=F32)


def dot_tn(a, b):
    return lax.dot_general(a, b, (((0,), (0,)), ((), ())), preferred_element_type=F32)


def kernel(n, ng, cap, block, len_ref, routes_ref, px_hbm, dx_hbm, w_hbm, pg_hbm, dg_hbm, cache_hbm, dtw_hbm,
           bias_ref, alog_ref, skip_ref, outp_ref, outd_ref,
           px, dx, w, pg, dg, cache, dtw, part, recv, full, low, lhs_c, lhs_b,
           decay, force, forced, hb, hs, mix, state_out, state_in,
           in_sem, send_sem, recv_sem, gsend_sem, grecv_sem, hsend_sem, hrecv_sem):
    me = lax.axis_index("tp")
    group = lax.axis_index("group")
    tokens, channels = px.shape
    steps, rows, _ = dx.shape
    rank = dtw.shape[0]
    states = alog_ref.shape[0]
    requests = len_ref.shape[1]
    blocks = channels // block
    piece = part.shape[2]
    slots = min(ng * cap, rows)

    loads = [
        pltpu.make_async_copy(src, dst, in_sem.at[i])
        for i, (src, dst) in enumerate(
            ((w_hbm, w), (px_hbm, px), (dx_hbm, dx), (dtw_hbm, dtw), (pg_hbm, pg), (cache_hbm, cache), (dg_hbm, dg))
        )
    ]
    for load in loads:
        load.start()
    barrier = pltpu.get_barrier_semaphore()
    for k in range(1, n):
        pl.semaphore_signal(barrier, inc=1, device_id={"tp": lax.rem(me + k, n)}, device_id_type=MESH)
    for k in range(1, ng):
        pl.semaphore_signal(barrier, inc=1, device_id={"group": lax.rem(group + k, ng)}, device_id_type=MESH)

    def scatter(phase, k):
        peer = lax.rem(me + k, n)
        return pltpu.make_async_remote_copy(
            src_ref=part.at[phase, peer],
            dst_ref=recv.at[phase, k - 1],
            send_sem=send_sem.at[phase, k - 1],
            recv_sem=recv_sem.at[phase, k - 1],
            device_id={"tp": peer},
            device_id_type=MESH,
        )

    def gather(phase, k, owner):
        return pltpu.make_async_remote_copy(
            src_ref=full.at[phase, owner],
            dst_ref=full.at[phase, owner],
            send_sem=gsend_sem.at[phase, k - 1],
            recv_sem=grecv_sem.at[phase, k - 1],
            device_id={"tp": lax.rem(me + k, n)},
            device_id_type=MESH,
        )

    def handoff(b, k):
        return pltpu.make_async_remote_copy(
            src_ref=state_out.at[b, k - 1],
            dst_ref=state_in.at[b, k],
            send_sem=hsend_sem.at[b, k - 1],
            recv_sem=hrecv_sem.at[b, k - 1],
            device_id={"group": lax.rem(group + k, ng)},
            device_id_type=MESH,
        )

    for phase in range(2):
        if phase == 0:
            loads[0].wait()
            loads[1].wait()
            values = px[...]
        else:
            loads[2].wait()
            values = dx[...].reshape(steps * rows, channels)
        res = dot_nt(w[...], values)
        for j in range(n):
            part[phase, j] = res[j * piece:(j + 1) * piece]
        if phase == 0:
            pl.semaphore_wait(barrier, n - 1 + ng - 1)
        for k in range(1, n):
            scatter(phase, k).start()

    ends = []
    at = jnp.int32(0)
    for k in range(requests):
        at = at + len_ref[0, k]
        ends.append(at)
    leaving = []
    for k in range(ng):
        dest = lax.rem(group + k, ng)
        found = [jnp.int32(0)] * cap
        count = jnp.int32(0)
        for q in range(requests):
            hit = routes_ref[group * requests + q, 0] == dest
            found = [jnp.where(hit & (count == r), jnp.maximum(ends[q] - 1, 0), found[r]) for r in range(cap)]
            count = count + hit.astype(jnp.int32)
        leaving.append(found)

    def locate(origin, carry):
        count, places = carry[0], list(carry[1:])
        arrived = jnp.int32(0)
        turn = lax.rem(group + ng - origin, ng)
        for q in range(requests):
            hit = routes_ref[origin * requests + q, 0] == group
            places = [jnp.where(hit & (count == r), turn * cap + arrived, places[r]) for r in range(slots)]
            count = count + hit.astype(jnp.int32)
            arrived = arrived + hit.astype(jnp.int32)
        return (count, *places)

    located = lax.fori_loop(0, ng, locate, (jnp.int32(0),) * (slots + 1))
    taken, places = located[0], located[1:]

    for phase in range(2):
        total = part[phase, me]
        for k in range(1, n):
            scatter(phase, k).wait_recv()
            total = total + recv[phase, k - 1]
        full[phase, me] = total
        for k in range(1, n):
            gather(phase, k, me).start()

    tile = (lax.broadcasted_iota(jnp.int32, (states, SET * states), 1) % states
            == lax.broadcasted_iota(jnp.int32, (states, SET * states), 0)).astype(F32)

    def collect(phase):
        for k in range(1, n):
            gather(phase, k, lax.rem(me + n - k, n)).wait_recv()
        proj = jnp.concatenate([full[phase, j] for j in range(n)], axis=0)
        low[phase] = proj[:rank].astype(BF16)
        width = proj.shape[1]
        spread_b = dot_tn(tile, proj[rank:rank + states])
        own = (lax.broadcasted_iota(jnp.int32, (SET * states, width), 0) // states
               == lax.broadcasted_iota(jnp.int32, (SET * states, width), 1) % SET)
        spread_b = jnp.where(own, spread_b, 0.0).astype(BF16)
        spread_c = dot_tn(proj[rank + states:], tile)
        own = (lax.broadcasted_iota(jnp.int32, (width, SET * states), 1) // states
               == lax.broadcasted_iota(jnp.int32, (width, SET * states), 0) % SET)
        lhs_c[phase] = jnp.where(own, spread_c, 0.0).astype(BF16)
        for s in range(width // SET):
            lhs_b[phase, s] = spread_b[:, s * SET:(s + 1) * SET]

    def step_sizes(phase, lanes):
        return softplus(dot_tn(low[phase], dtw[:, lanes]) + bias_ref[:, lanes])

    collect(0)
    loads[3].wait()
    loads[4].wait()
    position = lax.broadcasted_iota(jnp.int32, (tokens, block), 0)
    first = position == 0
    for k in range(requests - 1):
        first = first | (position == ends[k])

    def prefill_block(b, carry):
        lanes = pl.ds(pl.multiple_of(b * block, block), block)
        step = step_sizes(0, lanes)
        values = px[:, lanes].astype(F32)
        decay[...] = jnp.where(first, 1e30, step)
        force[...] = (step * values).astype(BF16)
        rates = -jnp.exp(alog_ref[:, lanes]) * LOG2E

        def some(s, h):
            base = pl.multiple_of(s * SET, SET)
            forced[0] = jnp.dot(lhs_b[0, s], force[pl.ds(base, SET), :], preferred_element_type=F32)
            for j in range(SET):
                da = jnp.exp2(decay[pl.ds(base + j, 1), :] * rates)
                h = da * h + forced[0, j * states:(j + 1) * states, :]
                hs[base + j] = h
                hb[0, j * states:(j + 1) * states, :] = h.astype(BF16)
            mix[pl.ds(base, SET), :] = jnp.dot(lhs_c[0, pl.ds(base, SET), :], hb[0], preferred_element_type=F32)
            return h

        lax.fori_loop(0, tokens // SET, some, jnp.zeros((states, block), F32))
        for k in range(1, ng):
            for r in range(cap):
                state_out[b, k - 1, r] = hs[leaving[k][r]]
            handoff(b, k).start()
        for r in range(cap):
            state_in[b, 0, r] = hs[leaving[0][r]]
        outp_ref[:, lanes] = ((mix[...] + skip_ref[:, lanes] * values) * silu(pg[:, lanes].astype(F32))).astype(BF16)
        return carry

    lax.fori_loop(0, blocks, prefill_block, 0)

    collect(1)
    loads[5].wait()
    loads[6].wait()

    def decode_rows(b, base, takes):
        lanes = pl.ds(pl.multiple_of(b * block, block), block)
        step = step_sizes(1, lanes).reshape(steps, rows, block)[:, base:base + SET]
        values = dx[:, base:base + SET, lanes].astype(F32)
        now = pl.ds(0, SET)
        for i in range(steps):
            decay[i * SET:(i + 1) * SET, :] = step[i]
            forced[i] = jnp.dot(lhs_b[1, (i * rows + base) // SET], (step[i] * values[i]).astype(BF16),
                                preferred_element_type=F32)
        rates = -jnp.exp(alog_ref[:, lanes]) * LOG2E
        for j in range(SET):
            row = base + j
            h = cache[row, :, lanes]
            if takes and row < slots:
                place = places[row]
                h = jnp.where(row < taken, hs[place], h)
            for i in range(steps):
                da = jnp.exp2(decay[i * SET + j:i * SET + j + 1, :] * rates)
                h = da * h + forced[i, j * states:(j + 1) * states, :]
                hb[i, j * states:(j + 1) * states, :] = h.astype(BF16)
        skip = skip_ref[:, lanes]
        for i in range(steps):
            at = i * rows + base
            mixed = jnp.dot(lhs_c[1, at:at + SET, :], hb[i], preferred_element_type=F32)
            gate = silu(dg[i, base:base + SET, lanes].astype(F32))
            outd_ref[i, base:base + SET, lanes] = ((mixed + skip * values[i]) * gate).astype(BF16)

    late = [base for base in range(0, rows, SET) if base < slots]
    early = [base for base in range(0, rows, SET) if base >= slots]

    def early_block(b, carry):
        for base in early:
            decode_rows(b, base, False)
        return carry

    def late_block(b, carry):
        for k in range(1, ng):
            handoff(b, k).wait_recv()
        for k in range(ng):
            for r in range(cap):
                hs[k * cap + r] = state_in[b, k, r]
        for base in late:
            decode_rows(b, base, True)
        return carry

    lax.fori_loop(0, blocks, early_block, 0)
    lax.fori_loop(0, blocks, late_block, 0)

    for phase in range(2):
        for k in range(1, n):
            scatter(phase, k).wait_send()
            gather(phase, k, me).wait_send()

    def finish(b, carry):
        for k in range(1, ng):
            handoff(b, k).wait_send()
        return carry

    lax.fori_loop(0, blocks, finish, 0)


def local(n, ng, prefill_x, prefill_gate, lengths, routes, decode_x, decode_gate, cached_state,
          xproj_weight, dt_weight, dt_bias, a_log, skip_gain):
    tokens, channels = prefill_x.shape
    steps, rows, _ = decode_x.shape
    rank, states = dt_weight.shape[0], a_log.shape[0]
    width = xproj_weight.shape[1]
    cap = max(1, 2 * lengths.shape[1] // ng)
    block = min(512, channels)
    blocks = channels // block
    piece = width // n
    columns = max(tokens, steps * rows)
    anywhere = pl.BlockSpec(memory_space=pl.ANY)
    smem = pl.BlockSpec(memory_space=pltpu.SMEM)
    vmem = pl.BlockSpec(memory_space=pltpu.VMEM)
    dma = pltpu.SemaphoreType.DMA
    return pl.pallas_call(
        functools.partial(kernel, n, ng, cap, block),
        out_shape=(
            jax.ShapeDtypeStruct(prefill_x.shape, BF16),
            jax.ShapeDtypeStruct(decode_x.shape, BF16),
        ),
        in_specs=[smem, smem] + [anywhere] * 7 + [vmem] * 3,
        out_specs=(vmem, vmem),
        scratch_shapes=[
            pltpu.VMEM(prefill_x.shape, BF16),
            pltpu.VMEM(decode_x.shape, BF16),
            pltpu.VMEM((width, channels), BF16),
            pltpu.VMEM(prefill_x.shape, BF16),
            pltpu.VMEM(decode_x.shape, BF16),
            pltpu.VMEM(cached_state.shape, F32),
            pltpu.VMEM(dt_weight.shape, BF16),
            pltpu.VMEM((2, n, piece, columns), F32),
            pltpu.VMEM((2, n - 1, piece, columns), F32),
            pltpu.VMEM((2, n, piece, columns), F32),
            pltpu.VMEM((2, rank, columns), BF16),
            pltpu.VMEM((2, columns, SET * states), BF16),
            pltpu.VMEM((2, columns // SET, SET * states, SET), BF16),
            pltpu.VMEM((columns, block), F32),
            pltpu.VMEM((columns, block), BF16),
            pltpu.VMEM((steps, SET * states, block), F32),
            pltpu.VMEM((steps, SET * states, block), BF16),
            pltpu.VMEM((tokens, states, block), F32),
            pltpu.VMEM((tokens, block), F32),
            pltpu.VMEM((blocks, ng - 1, cap, states, block), F32),
            pltpu.VMEM((blocks, ng, cap, states, block), F32),
            dma((7,)),
            dma((2, n - 1)),
            dma((2, n - 1)),
            dma((2, n - 1)),
            dma((2, n - 1)),
            dma((blocks, ng - 1)),
            dma((blocks, ng - 1)),
        ],
        compiler_params=pltpu.CompilerParams(
            collective_id=0, has_side_effects=True, vmem_limit_bytes=52 * 1024 * 1024
        ),
        name="layer",
    )(lengths, routes, prefill_x, decode_x, xproj_weight.T, prefill_gate, decode_gate, cached_state, dt_weight,
      dt_bias[None], a_log, skip_gain[None])


def solution(mesh):
    placed = (
        P("group", "tp"),
        P("group", "tp"),
        P("group", None),
        P(),
        P(None, "group", "tp"),
        P(None, "group", "tp"),
        P("group", None, "tp"),
        P("tp", None),
        P(None, "tp"),
        P("tp"),
        P(None, "tp"),
        P("tp"),
    )
    return jax.shard_map(
        functools.partial(local, mesh.shape["tp"], mesh.shape["group"]),
        mesh=mesh,
        in_specs=placed,
        out_specs=(P("group", "tp"), P(None, "group", "tp")),
        check_vma=False,
    )
```

```python
import functools
import jax
import jax.numpy as jnp
from jax import lax
from jax.experimental import pallas as pl
from jax.experimental.pallas import tpu as pltpu
from jax.sharding import PartitionSpec as P

MESH = pl.DeviceIdType.MESH
F32 = jnp.float32
BF16 = jnp.bfloat16
LOG2E = 1.4426950408889634
SET = 16


def softplus(v):
    return jnp.maximum(v, 0.0) + jnp.log1p(jnp.exp(-jnp.abs(v)))


def silu(v):
    return v / (1.0 + jnp.exp(-v))


def dot_nt(a, b):
    return lax.dot_general(a, b, (((1,), (1,)), ((), ())), preferred_element_type=F32)


def dot_tn(a, b):
    return lax.dot_general(a, b, (((0,), (0,)), ((), ())), preferred_element_type=F32)


def halves(v):
    high = v.astype(BF16)
    return high, (v - high.astype(F32)).astype(BF16)


def kernel(n, ng, cap, block, len_hbm, routes_hbm, px_hbm, dx_hbm, w_hbm, pg_hbm, dg_hbm, cache_hbm, dtw_hbm,
           bias_hbm, alog_hbm, skip_hbm, outp_ref, outd_ref,
           len_ref, routes_ref, bias_ref, alog_ref, skip_ref,
           px, dx, w, pg, dg, cache, dtw, part, recv, full, low, lhs_c, lhs_b,
           decay, force, forced, hb, hd, mix, state_out, state_in, pool,
           in_sem, send_sem, recv_sem, gsend_sem, grecv_sem, hsend_sem, hrecv_sem):
    me = lax.axis_index("tp")
    group = lax.axis_index("group")
    tokens, channels = px.shape
    steps, rows, _ = dx.shape
    rank = dtw.shape[0]
    states = alog_ref.shape[0]
    requests = len_ref.shape[1]
    blocks = channels // block
    piece = part.shape[2]
    slots = min(ng * cap, rows)

    loads = [
        pltpu.make_async_copy(src, dst, in_sem.at[i])
        for i, (src, dst) in enumerate(
            ((w_hbm, w), (px_hbm, px), (dx_hbm, dx), (dtw_hbm, dtw), (pg_hbm, pg), (cache_hbm, cache), (dg_hbm, dg),
             (len_hbm, len_ref), (routes_hbm, routes_ref), (bias_hbm, bias_ref), (alog_hbm, alog_ref),
             (skip_hbm, skip_ref))
        )
    ]
    for load in loads:
        load.start()
    barrier = pltpu.get_barrier_semaphore()
    for k in range(1, n):
        pl.semaphore_signal(barrier, inc=1, device_id={"tp": lax.rem(me + k, n)}, device_id_type=MESH)
    for k in range(1, ng):
        pl.semaphore_signal(barrier, inc=1, device_id={"group": lax.rem(group + k, ng)}, device_id_type=MESH)

    def scatter(phase, k):
        peer = lax.rem(me + k, n)
        return pltpu.make_async_remote_copy(
            src_ref=part.at[phase, peer],
            dst_ref=recv.at[phase, k - 1],
            send_sem=send_sem.at[phase, k - 1],
            recv_sem=recv_sem.at[phase, k - 1],
            device_id={"tp": peer},
            device_id_type=MESH,
        )

    def gather(phase, k, owner):
        return pltpu.make_async_remote_copy(
            src_ref=full.at[phase, owner],
            dst_ref=full.at[phase, owner],
            send_sem=gsend_sem.at[phase, k - 1],
            recv_sem=grecv_sem.at[phase, k - 1],
            device_id={"tp": lax.rem(me + k, n)},
            device_id_type=MESH,
        )

    def handoff(b, k):
        return pltpu.make_async_remote_copy(
            src_ref=state_out.at[b, k - 1],
            dst_ref=state_in.at[b, k],
            send_sem=hsend_sem.at[b, k - 1],
            recv_sem=hrecv_sem.at[b, k - 1],
            device_id={"group": lax.rem(group + k, ng)},
            device_id_type=MESH,
        )

    for phase in range(2):
        if phase == 0:
            loads[0].wait()
            loads[1].wait()
            values = px[...]
        else:
            loads[2].wait()
            values = dx[...].reshape(steps * rows, channels)
        res = dot_nt(w[...], values)
        for j in range(n):
            part[phase, j] = res[j * piece:(j + 1) * piece]
        if phase == 0:
            pl.semaphore_wait(barrier, n - 1 + ng - 1)
            for k in range(1, n):
                scatter(phase, k).start()
    for i in range(7, 12):
        loads[i].wait()

    ends = []
    at = jnp.int32(0)
    for k in range(requests):
        at = at + len_ref[0, k]
        ends.append(at)
    leaving = []
    for k in range(ng):
        dest = lax.rem(group + k, ng)
        found = [jnp.int32(0)] * cap
        count = jnp.int32(0)
        for q in range(requests):
            hit = routes_ref[0, group * requests + q] == dest
            found = [jnp.where(hit & (count == r), jnp.maximum(ends[q] - 1, 0), found[r]) for r in range(cap)]
            count = count + hit.astype(jnp.int32)
        leaving.append(found)

    def locate(origin, carry):
        count, places = carry[0], list(carry[1:])
        arrived = jnp.int32(0)
        turn = lax.rem(group + ng - origin, ng)
        for q in range(requests):
            hit = routes_ref[0, origin * requests + q] == group
            places = [jnp.where(hit & (count == r), turn * cap + arrived, places[r]) for r in range(slots)]
            count = count + hit.astype(jnp.int32)
            arrived = arrived + hit.astype(jnp.int32)
        return (count, *places)

    located = lax.fori_loop(0, ng, locate, (jnp.int32(0),) * (slots + 1))
    taken, places = located[0], located[1:]

    def reduce(phase):
        total = part[phase, me]
        for k in range(1, n):
            scatter(phase, k).wait_recv()
            total = total + recv[phase, k - 1]
        full[phase, me] = total
        for k in range(1, n):
            gather(phase, k, me).start()

    reduce(0)
    for k in range(1, n):
        scatter(1, k).start()

    tile = (lax.broadcasted_iota(jnp.int32, (states, SET * states), 1) % states
            == lax.broadcasted_iota(jnp.int32, (states, SET * states), 0)).astype(BF16)

    def collect(phase):
        for k in range(1, n):
            gather(phase, k, lax.rem(me + n - k, n)).wait_recv()
        proj = jnp.concatenate([full[phase, j] for j in range(n)], axis=0)
        low[phase] = proj[:rank].astype(BF16)
        width = proj.shape[1]
        own = (lax.broadcasted_iota(jnp.int32, (SET * states, width), 0) // states
               == lax.broadcasted_iota(jnp.int32, (SET * states, width), 1) % SET)
        high, rest = [jnp.where(own, dot_tn(tile, v), 0.0).astype(BF16) for v in halves(proj[rank:rank + states])]
        for s in range(width // SET):
            lhs_b[phase, s] = jnp.concatenate([v[:, s * SET:(s + 1) * SET] for v in (high, rest, high)], axis=1)
        own = (lax.broadcasted_iota(jnp.int32, (width, SET * states), 1) // states
               == lax.broadcasted_iota(jnp.int32, (width, SET * states), 0) % SET)
        high, rest = [jnp.where(own, dot_tn(v, tile), 0.0).astype(BF16) for v in halves(proj[rank + states:])]
        for s in range(width // SET):
            lhs_c[phase, s, :SET] = high[s * SET:(s + 1) * SET]
            lhs_c[phase, s, SET:] = rest[s * SET:(s + 1) * SET]

    def forcing(phase, s, values):
        high, rest = halves(values)
        return jnp.dot(lhs_b[phase, s], jnp.concatenate([high, high, rest], axis=0), preferred_element_type=F32)

    def readout(phase, s, hidden):
        both = jnp.dot(lhs_c[phase, s], hidden.reshape(SET * states, block), preferred_element_type=F32)
        return both[:SET] + both[SET:]

    def step_sizes(phase, lanes):
        return softplus(dot_tn(low[phase], dtw[:, lanes]) + bias_ref[:, lanes])

    collect(0)
    loads[3].wait()
    loads[4].wait()
    position = lax.broadcasted_iota(jnp.int32, (tokens, block), 0)
    first = position == 0
    for k in range(requests - 1):
        first = first | (position == ends[k])

    def prefill_block(b, carry):
        lanes = pl.ds(pl.multiple_of(b * block, block), block)
        step = step_sizes(0, lanes)
        values = px[:, lanes].astype(F32)
        decay[...] = jnp.where(first, 1e30, step)
        force[...] = step * values
        rates = -jnp.exp(alog_ref[:, lanes]) * LOG2E

        def some(s, h):
            base = pl.multiple_of(s * SET, SET)
            forced[0] = forcing(0, s, force[pl.ds(base, SET), :])
            for j in range(SET):
                da = jnp.exp2(decay[pl.ds(base + j, 1), :] * rates)
                h = da * h + forced[0, j * states:(j + 1) * states, :]
                hb[base + j] = h.astype(BF16)
            mix[pl.ds(base, SET), :] = readout(0, s, hb[pl.ds(base, SET)])
            return h

        lax.fori_loop(0, tokens // SET, some, jnp.zeros((states, block), F32))
        for k in range(1, ng):
            for r in range(cap):
                state_out[b, k - 1, r] = hb[leaving[k][r]].astype(F32)
            handoff(b, k).start()
        for r in range(cap):
            state_in[b, 0, r] = hb[leaving[0][r]].astype(F32)
        outp_ref[:, lanes] = ((mix[...] + skip_ref[:, lanes] * values) * silu(pg[:, lanes].astype(F32))).astype(BF16)
        return carry

    lax.fori_loop(0, blocks // 2, prefill_block, 0)
    reduce(1)
    lax.fori_loop(blocks // 2, blocks, prefill_block, 0)

    collect(1)
    loads[5].wait()
    loads[6].wait()

    def decode_rows(b, base, takes):
        lanes = pl.ds(pl.multiple_of(b * block, block), block)
        step = step_sizes(1, lanes).reshape(steps, rows, block)[:, base:base + SET]
        values = dx[:, base:base + SET, lanes].astype(F32)
        now = pl.ds(0, SET)
        for i in range(steps):
            decay[i * SET:(i + 1) * SET, :] = step[i]
            forced[i] = forcing(1, (i * rows + base) // SET, step[i] * values[i])
        rates = -jnp.exp(alog_ref[:, lanes]) * LOG2E
        for j in range(SET):
            row = base + j
            h = cache[row, :, lanes]
            if takes and row < slots:
                place = places[row]
                h = jnp.where(row < taken, pool[place], h)
            for i in range(steps):
                da = jnp.exp2(decay[i * SET + j:i * SET + j + 1, :] * rates)
                h = da * h + forced[i, j * states:(j + 1) * states, :]
                hd[i, j] = h.astype(BF16)
        skip = skip_ref[:, lanes]
        for i in range(steps):
            mixed = readout(1, (i * rows + base) // SET, hd[i])
            gate = silu(dg[i, base:base + SET, lanes].astype(F32))
            outd_ref[i, base:base + SET, lanes] = ((mixed + skip * values[i]) * gate).astype(BF16)

    late = [base for base in range(0, rows, SET) if base < slots]
    early = [base for base in range(0, rows, SET) if base >= slots]

    def early_block(b, carry):
        for base in early:
            decode_rows(b, base, False)
        return carry

    def late_block(b, carry):
        for k in range(1, ng):
            handoff(b, k).wait_recv()
        for k in range(ng):
            for r in range(cap):
                pool[k * cap + r] = state_in[b, k, r]
        for base in late:
            decode_rows(b, base, True)
        return carry

    lax.fori_loop(0, blocks, early_block, 0)
    lax.fori_loop(0, blocks, late_block, 0)

    for phase in range(2):
        for k in range(1, n):
            scatter(phase, k).wait_send()
            gather(phase, k, me).wait_send()

    def finish(b, carry):
        for k in range(1, ng):
            handoff(b, k).wait_send()
        return carry

    lax.fori_loop(0, blocks, finish, 0)


def local(n, ng, prefill_x, prefill_gate, lengths, routes, decode_x, decode_gate, cached_state,
          xproj_weight, dt_weight, dt_bias, a_log, skip_gain):
    tokens, channels = prefill_x.shape
    steps, rows, _ = decode_x.shape
    rank, states = dt_weight.shape[0], a_log.shape[0]
    width = xproj_weight.shape[1]
    cap = max(1, 2 * lengths.shape[1] // ng)
    block = min(512, channels)
    blocks = channels // block
    piece = width // n
    columns = max(tokens, steps * rows)
    anywhere = pl.BlockSpec(memory_space=pltpu.HBM)
    vmem = pl.BlockSpec(memory_space=pltpu.VMEM)
    dma = pltpu.SemaphoreType.DMA
    return pl.pallas_call(
        functools.partial(kernel, n, ng, cap, block),
        out_shape=(
            jax.ShapeDtypeStruct(prefill_x.shape, BF16),
            jax.ShapeDtypeStruct(decode_x.shape, BF16),
        ),
        in_specs=[anywhere] * 12,
        out_specs=(vmem, vmem),
        scratch_shapes=[
            pltpu.SMEM(lengths.shape, jnp.int32),
            pltpu.SMEM((1, routes.shape[0]), jnp.int32),
            pltpu.VMEM((1, channels), F32),
            pltpu.VMEM(a_log.shape, F32),
            pltpu.VMEM((1, channels), F32),
            pltpu.VMEM(prefill_x.shape, BF16),
            pltpu.VMEM(decode_x.shape, BF16),
            pltpu.VMEM((width, channels), BF16),
            pltpu.VMEM(prefill_x.shape, BF16),
            pltpu.VMEM(decode_x.shape, BF16),
            pltpu.VMEM(cached_state.shape, F32),
            pltpu.VMEM(dt_weight.shape, BF16),
            pltpu.VMEM((2, n, piece, columns), F32),
            pltpu.VMEM((2, n - 1, piece, columns), F32),
            pltpu.VMEM((2, n, piece, columns), F32),
            pltpu.VMEM((2, rank, columns), BF16),
            pltpu.VMEM((2, columns // SET, 2 * SET, SET * states), BF16),
            pltpu.VMEM((2, columns // SET, SET * states, 3 * SET), BF16),
            pltpu.VMEM((columns, block), F32),
            pltpu.VMEM((columns, block), F32),
            pltpu.VMEM((steps, SET * states, block), F32),
            pltpu.VMEM((tokens, states, block), BF16),
            pltpu.VMEM((steps, SET, states, block), BF16),
            pltpu.VMEM((tokens, block), F32),
            pltpu.VMEM((blocks, ng - 1, cap, states, block), F32),
            pltpu.VMEM((blocks, ng, cap, states, block), F32),
            pltpu.VMEM((ng * cap + lengths.shape[1], states, block), F32),
            dma((12,)),
            dma((2, n - 1)),
            dma((2, n - 1)),
            dma((2, n - 1)),
            dma((2, n - 1)),
            dma((blocks, ng - 1)),
            dma((blocks, ng - 1)),
        ],
        compiler_params=pltpu.CompilerParams(
            collective_id=0, has_side_effects=True, vmem_limit_bytes=52 * 1024 * 1024
        ),
        name="layer",
    )(lengths, routes.T, prefill_x, decode_x, xproj_weight.T, prefill_gate, decode_gate, cached_state, dt_weight,
      dt_bias[None], a_log, skip_gain[None])


def solution(mesh):
    placed = (
        P("group", "tp"),
        P("group", "tp"),
        P("group", None),
        P(),
        P(None, "group", "tp"),
        P(None, "group", "tp"),
        P("group", None, "tp"),
        P("tp", None),
        P(None, "tp"),
        P("tp"),
        P(None, "tp"),
        P("tp"),
    )
    return jax.shard_map(
        functools.partial(local, mesh.shape["tp"], mesh.shape["group"]),
        mesh=mesh,
        in_specs=placed,
        out_specs=(P("group", "tp"), P(None, "group", "tp")),
        check_vma=False,
    )
```

```python
import functools
import jax
import jax.numpy as jnp
from jax import lax
from jax.experimental import pallas as pl
from jax.experimental.pallas import tpu as pltpu
from jax.sharding import PartitionSpec as P

MESH = pl.DeviceIdType.MESH
F32 = jnp.float32
BF16 = jnp.bfloat16
LOG2E = 1.4426950408889634
SET = 16


def softplus(v):
    return jnp.maximum(v, 0.0) + jnp.log1p(jnp.exp(-jnp.abs(v)))


def silu(v):
    return v / (1.0 + jnp.exp(-v))


def dot_nt(a, b):
    return lax.dot_general(a, b, (((1,), (1,)), ((), ())), preferred_element_type=F32)


def dot_tn(a, b):
    return lax.dot_general(a, b, (((0,), (0,)), ((), ())), preferred_element_type=F32)


def halves(v):
    high = v.astype(BF16)
    return high, (v - high.astype(F32)).astype(BF16)


def kernel(n, ng, cap, block, len_hbm, routes_hbm, px_hbm, dx_hbm, w_hbm, pg_hbm, dg_hbm, cache_hbm, dtw_hbm,
           bias_hbm, alog_hbm, skip_hbm, outp_ref, outd_ref,
           len_ref, routes_ref, bias_ref, alog_ref, skip_ref,
           px, dx, w, pg, dg, cache, dtw, part, recv, full, low, lhs_c, lhs_b,
           decay, force, forced, hb, hd, mix, state_out, state_in, pool,
           in_sem, send_sem, recv_sem, gsend_sem, grecv_sem, hsend_sem, hrecv_sem):
    me = lax.axis_index("tp")
    group = lax.axis_index("group")
    tokens, channels = px.shape
    steps, rows, _ = dx.shape
    rank = dtw.shape[0]
    states = alog_ref.shape[0]
    requests = len_ref.shape[1]
    blocks = channels // block
    piece = part.shape[2]
    slots = min(ng * cap, rows)

    loads = [
        pltpu.make_async_copy(src, dst, in_sem.at[i])
        for i, (src, dst) in enumerate(
            ((w_hbm, w), (px_hbm, px), (dx_hbm, dx), (dtw_hbm, dtw), (pg_hbm, pg), (cache_hbm, cache), (dg_hbm, dg),
             (len_hbm, len_ref), (routes_hbm, routes_ref), (bias_hbm, bias_ref), (alog_hbm, alog_ref),
             (skip_hbm, skip_ref))
        )
    ]
    for i in (0, 1, 2, 7, 8, 9, 10, 11):
        loads[i].start()
    barrier = pltpu.get_barrier_semaphore()
    for k in range(1, n):
        pl.semaphore_signal(barrier, inc=1, device_id={"tp": lax.rem(me + k, n)}, device_id_type=MESH)
    for k in range(1, ng):
        pl.semaphore_signal(barrier, inc=1, device_id={"group": lax.rem(group + k, ng)}, device_id_type=MESH)

    def scatter(phase, k):
        peer = lax.rem(me + k, n)
        return pltpu.make_async_remote_copy(
            src_ref=part.at[phase, peer],
            dst_ref=recv.at[phase, k - 1],
            send_sem=send_sem.at[phase, k - 1],
            recv_sem=recv_sem.at[phase, k - 1],
            device_id={"tp": peer},
            device_id_type=MESH,
        )

    def gather(phase, k, owner):
        return pltpu.make_async_remote_copy(
            src_ref=full.at[phase, owner],
            dst_ref=full.at[phase, owner],
            send_sem=gsend_sem.at[phase, k - 1],
            recv_sem=grecv_sem.at[phase, k - 1],
            device_id={"tp": lax.rem(me + k, n)},
            device_id_type=MESH,
        )

    def handoff(b, k):
        return pltpu.make_async_remote_copy(
            src_ref=state_out.at[b, k - 1],
            dst_ref=state_in.at[b, k],
            send_sem=hsend_sem.at[b, k - 1],
            recv_sem=hrecv_sem.at[b, k - 1],
            device_id={"group": lax.rem(group + k, ng)},
            device_id_type=MESH,
        )

    for phase in range(2):
        if phase == 0:
            loads[0].wait()
            loads[1].wait()
            values = px[...]
        else:
            loads[2].wait()
            values = dx[...].reshape(steps * rows, channels)
        res = dot_nt(w[...], values)
        for j in range(n):
            part[phase, j] = res[j * piece:(j + 1) * piece]
        if phase == 0:
            pl.semaphore_wait(barrier, n - 1 + ng - 1)
            for k in range(1, n):
                scatter(phase, k).start()
            for i in (3, 4, 5, 6):
                loads[i].start()
    for i in range(7, 12):
        loads[i].wait()

    ends = []
    at = jnp.int32(0)
    for k in range(requests):
        at = at + len_ref[0, k]
        ends.append(at)
    leaving = []
    for k in range(ng):
        dest = lax.rem(group + k, ng)
        found = [jnp.int32(0)] * cap
        count = jnp.int32(0)
        for q in range(requests):
            hit = routes_ref[0, group * requests + q] == dest
            found = [jnp.where(hit & (count == r), jnp.maximum(ends[q] - 1, 0), found[r]) for r in range(cap)]
            count = count + hit.astype(jnp.int32)
        leaving.append(found)

    def locate(origin, carry):
        count, places = carry[0], list(carry[1:])
        arrived = jnp.int32(0)
        turn = lax.rem(group + ng - origin, ng)
        for q in range(requests):
            hit = routes_ref[0, origin * requests + q] == group
            places = [jnp.where(hit & (count == r), turn * cap + arrived, places[r]) for r in range(slots)]
            count = count + hit.astype(jnp.int32)
            arrived = arrived + hit.astype(jnp.int32)
        return (count, *places)

    located = lax.fori_loop(0, ng, locate, (jnp.int32(0),) * (slots + 1))
    taken, places = located[0], located[1:]

    def reduce(phase):
        total = part[phase, me]
        for k in range(1, n):
            scatter(phase, k).wait_recv()
            total = total + recv[phase, k - 1]
        full[phase, me] = total
        for k in range(1, n):
            gather(phase, k, me).start()

    reduce(0)
    for k in range(1, n):
        scatter(1, k).start()

    tile = (lax.broadcasted_iota(jnp.int32, (states, SET * states), 1) % states
            == lax.broadcasted_iota(jnp.int32, (states, SET * states), 0)).astype(BF16)

    def collect(phase):
        for k in range(1, n):
            gather(phase, k, lax.rem(me + n - k, n)).wait_recv()
        proj = jnp.concatenate([full[phase, j] for j in range(n)], axis=0)
        low[phase] = proj[:rank].astype(BF16)
        width = proj.shape[1]
        own = (lax.broadcasted_iota(jnp.int32, (SET * states, width), 0) // states
               == lax.broadcasted_iota(jnp.int32, (SET * states, width), 1) % SET)
        high, rest = [jnp.where(own, dot_tn(tile, v), 0.0).astype(BF16) for v in halves(proj[rank:rank + states])]
        for s in range(width // SET):
            lhs_b[phase, s] = jnp.concatenate([v[:, s * SET:(s + 1) * SET] for v in (high, rest, high)], axis=1)
        own = (lax.broadcasted_iota(jnp.int32, (width, SET * states), 1) // states
               == lax.broadcasted_iota(jnp.int32, (width, SET * states), 0) % SET)
        high, rest = [jnp.where(own, dot_tn(v, tile), 0.0).astype(BF16) for v in halves(proj[rank + states:])]
        for s in range(width // SET):
            lhs_c[phase, s, :SET] = high[s * SET:(s + 1) * SET]
            lhs_c[phase, s, SET:] = rest[s * SET:(s + 1) * SET]

    def forcing(phase, s, values):
        high, rest = halves(values)
        return jnp.dot(lhs_b[phase, s], jnp.concatenate([high, high, rest], axis=0), preferred_element_type=F32)

    def readout(phase, s, hidden):
        both = jnp.dot(lhs_c[phase, s], hidden.reshape(SET * states, block), preferred_element_type=F32)
        return both[:SET] + both[SET:]

    def step_sizes(phase, lanes):
        return softplus(dot_tn(low[phase], dtw[:, lanes]) + bias_ref[:, lanes])

    collect(0)
    loads[3].wait()
    loads[4].wait()
    position = lax.broadcasted_iota(jnp.int32, (tokens, block), 0)
    first = position == 0
    for k in range(requests - 1):
        first = first | (position == ends[k])

    def prefill_block(b, carry):
        lanes = pl.ds(pl.multiple_of(b * block, block), block)
        step = step_sizes(0, lanes)
        values = px[:, lanes].astype(F32)
        decay[...] = jnp.where(first, 1e30, step)
        force[...] = step * values
        rates = -jnp.exp(alog_ref[:, lanes]) * LOG2E

        def some(s, h):
            base = pl.multiple_of(s * SET, SET)
            forced[0] = forcing(0, s, force[pl.ds(base, SET), :])
            for j in range(SET):
                da = jnp.exp2(decay[pl.ds(base + j, 1), :] * rates)
                h = da * h + forced[0, j * states:(j + 1) * states, :]
                hb[base + j] = h.astype(BF16)
            mix[pl.ds(base, SET), :] = readout(0, s, hb[pl.ds(base, SET)])
            return h

        lax.fori_loop(0, tokens // SET, some, jnp.zeros((states, block), F32))
        for k in range(1, ng):
            for r in range(cap):
                state_out[b, k - 1, r] = hb[leaving[k][r]].astype(F32)
            handoff(b, k).start()
        for r in range(cap):
            state_in[b, 0, r] = hb[leaving[0][r]].astype(F32)
        outp_ref[:, lanes] = ((mix[...] + skip_ref[:, lanes] * values) * silu(pg[:, lanes].astype(F32))).astype(BF16)
        return carry

    lax.fori_loop(0, blocks // 2, prefill_block, 0)
    reduce(1)
    lax.fori_loop(blocks // 2, blocks, prefill_block, 0)

    collect(1)
    loads[5].wait()
    loads[6].wait()

    def decode_rows(b, base, takes):
        lanes = pl.ds(pl.multiple_of(b * block, block), block)
        step = step_sizes(1, lanes).reshape(steps, rows, block)[:, base:base + SET]
        values = dx[:, base:base + SET, lanes].astype(F32)
        now = pl.ds(0, SET)
        for i in range(steps):
            decay[i * SET:(i + 1) * SET, :] = step[i]
            forced[i] = forcing(1, (i * rows + base) // SET, step[i] * values[i])
        rates = -jnp.exp(alog_ref[:, lanes]) * LOG2E
        if takes and base == 0:
            for k in range(1, ng):
                handoff(b, k).wait_recv()
            for k in range(ng):
                for r in range(cap):
                    pool[k * cap + r] = state_in[b, k, r]
        for j in range(SET):
            row = base + j
            h = cache[row, :, lanes]
            if takes and row < slots:
                place = places[row]
                h = jnp.where(row < taken, pool[place], h)
            for i in range(steps):
                da = jnp.exp2(decay[i * SET + j:i * SET + j + 1, :] * rates)
                h = da * h + forced[i, j * states:(j + 1) * states, :]
                hd[i, j] = h.astype(BF16)
        skip = skip_ref[:, lanes]
        for i in range(steps):
            mixed = readout(1, (i * rows + base) // SET, hd[i])
            gate = silu(dg[i, base:base + SET, lanes].astype(F32))
            outd_ref[i, base:base + SET, lanes] = ((mixed + skip * values[i]) * gate).astype(BF16)

    late = [base for base in range(0, rows, SET) if base < slots]
    early = [base for base in range(0, rows, SET) if base >= slots]

    def early_block(b, carry):
        for base in early:
            decode_rows(b, base, False)
        return carry

    def late_block(b, carry):
        for base in late:
            decode_rows(b, base, True)
        return carry

    lax.fori_loop(0, blocks, early_block, 0)
    lax.fori_loop(0, blocks, late_block, 0)

    for phase in range(2):
        for k in range(1, n):
            scatter(phase, k).wait_send()
            gather(phase, k, me).wait_send()

    def finish(b, carry):
        for k in range(1, ng):
            handoff(b, k).wait_send()
        return carry

    lax.fori_loop(0, blocks, finish, 0)


def local(n, ng, prefill_x, prefill_gate, lengths, routes, decode_x, decode_gate, cached_state,
          xproj_weight, dt_weight, dt_bias, a_log, skip_gain):
    tokens, channels = prefill_x.shape
    steps, rows, _ = decode_x.shape
    rank, states = dt_weight.shape[0], a_log.shape[0]
    width = xproj_weight.shape[1]
    cap = max(1, 2 * lengths.shape[1] // ng)
    block = min(256, channels)
    blocks = channels // block
    piece = width // n
    columns = max(tokens, steps * rows)
    anywhere = pl.BlockSpec(memory_space=pltpu.HBM)
    vmem = pl.BlockSpec(memory_space=pltpu.VMEM)
    dma = pltpu.SemaphoreType.DMA
    return pl.pallas_call(
        functools.partial(kernel, n, ng, cap, block),
        out_shape=(
            jax.ShapeDtypeStruct(prefill_x.shape, BF16),
            jax.ShapeDtypeStruct(decode_x.shape, BF16),
        ),
        in_specs=[anywhere] * 12,
        out_specs=(vmem, vmem),
        scratch_shapes=[
            pltpu.SMEM(lengths.shape, jnp.int32),
            pltpu.SMEM((1, routes.shape[0]), jnp.int32),
            pltpu.VMEM((1, channels), F32),
            pltpu.VMEM(a_log.shape, F32),
            pltpu.VMEM((1, channels), F32),
            pltpu.VMEM(prefill_x.shape, BF16),
            pltpu.VMEM(decode_x.shape, BF16),
            pltpu.VMEM((width, channels), BF16),
            pltpu.VMEM(prefill_x.shape, BF16),
            pltpu.VMEM(decode_x.shape, BF16),
            pltpu.VMEM(cached_state.shape, F32),
            pltpu.VMEM(dt_weight.shape, BF16),
            pltpu.VMEM((2, n, piece, columns), F32),
            pltpu.VMEM((2, n - 1, piece, columns), F32),
            pltpu.VMEM((2, n, piece, columns), F32),
            pltpu.VMEM((2, rank, columns), BF16),
            pltpu.VMEM((2, columns // SET, 2 * SET, SET * states), BF16),
            pltpu.VMEM((2, columns // SET, SET * states, 3 * SET), BF16),
            pltpu.VMEM((columns, block), F32),
            pltpu.VMEM((columns, block), F32),
            pltpu.VMEM((steps, SET * states, block), F32),
            pltpu.VMEM((tokens, states, block), BF16),
            pltpu.VMEM((steps, SET, states, block), BF16),
            pltpu.VMEM((tokens, block), F32),
            pltpu.VMEM((blocks, ng - 1, cap, states, block), F32),
            pltpu.VMEM((blocks, ng, cap, states, block), F32),
            pltpu.VMEM((ng * cap + lengths.shape[1], states, block), F32),
            dma((12,)),
            dma((2, n - 1)),
            dma((2, n - 1)),
            dma((2, n - 1)),
            dma((2, n - 1)),
            dma((blocks, ng - 1)),
            dma((blocks, ng - 1)),
        ],
        compiler_params=pltpu.CompilerParams(
            collective_id=0, has_side_effects=True, vmem_limit_bytes=63 * 1024 * 1024
        ),
        name="layer",
    )(lengths, routes.T, prefill_x, decode_x, xproj_weight.T, prefill_gate, decode_gate, cached_state, dt_weight,
      dt_bias[None], a_log, skip_gain[None])


def solution(mesh):
    placed = (
        P("group", "tp"),
        P("group", "tp"),
        P("group", None),
        P(),
        P(None, "group", "tp"),
        P(None, "group", "tp"),
        P("group", None, "tp"),
        P("tp", None),
        P(None, "tp"),
        P("tp"),
        P(None, "tp"),
        P("tp"),
    )
    return jax.shard_map(
        functools.partial(local, mesh.shape["tp"], mesh.shape["group"]),
        mesh=mesh,
        in_specs=placed,
        out_specs=(P("group", "tp"), P(None, "group", "tp")),
        check_vma=False,
    )
```

```python
import functools
import jax
import jax.numpy as jnp
from jax import lax
from jax.experimental import pallas as pl
from jax.experimental.pallas import tpu as pltpu
from jax.sharding import PartitionSpec as P

MESH = pl.DeviceIdType.MESH
F32 = jnp.float32
BF16 = jnp.bfloat16
LOG2E = 1.4426950408889634
SET = 16


def softplus(v):
    return jnp.maximum(v, 0.0) + jnp.log1p(jnp.exp(-jnp.abs(v)))


def silu(v):
    return v / (1.0 + jnp.exp(-v))


def dot_nt(a, b):
    return lax.dot_general(a, b, (((1,), (1,)), ((), ())), preferred_element_type=F32)


def dot_tn(a, b):
    return lax.dot_general(a, b, (((0,), (0,)), ((), ())), preferred_element_type=F32)


def halves(v):
    high = v.astype(BF16)
    return high, (v - high.astype(F32)).astype(BF16)


def kernel(n, ng, cap, block, len_hbm, routes_hbm, px_hbm, dx_hbm, w_hbm, pg_hbm, dg_hbm, cache_hbm, dtw_hbm,
           bias_hbm, alog_hbm, skip_hbm, outp_ref, outd_ref,
           len_ref, routes_ref, bias_ref, alog_ref, skip_ref,
           px, dx, w, pg, dg, cache, dtw, part, recv, full, low, lhs_c, lhs_b,
           decay, forced, hb, hd, state_out, state_in, pool,
           in_sem, send_sem, recv_sem, gsend_sem, grecv_sem, hsend_sem, hrecv_sem):
    me = lax.axis_index("tp")
    group = lax.axis_index("group")
    tokens, channels = px.shape
    steps, rows, _ = dx.shape
    rank = dtw.shape[0]
    states = alog_ref.shape[0]
    requests = len_ref.shape[1]
    blocks = channels // block
    piece = part.shape[2]
    slots = min(ng * cap, rows)

    loads = [
        pltpu.make_async_copy(src, dst, in_sem.at[i])
        for i, (src, dst) in enumerate(
            ((w_hbm, w), (px_hbm, px), (dx_hbm, dx), (dtw_hbm, dtw), (pg_hbm, pg), (cache_hbm, cache), (dg_hbm, dg),
             (len_hbm, len_ref), (routes_hbm, routes_ref), (bias_hbm, bias_ref), (alog_hbm, alog_ref),
             (skip_hbm, skip_ref))
        )
    ]
    for i in (0, 1, 2, 7, 8, 9, 10, 11):
        loads[i].start()
    barrier = pltpu.get_barrier_semaphore()
    for k in range(1, n):
        pl.semaphore_signal(barrier, inc=1, device_id={"tp": lax.rem(me + k, n)}, device_id_type=MESH)
    for k in range(1, ng):
        pl.semaphore_signal(barrier, inc=1, device_id={"group": lax.rem(group + k, ng)}, device_id_type=MESH)

    def scatter(phase, k):
        peer = lax.rem(me + k, n)
        return pltpu.make_async_remote_copy(
            src_ref=part.at[phase, peer],
            dst_ref=recv.at[phase, k - 1],
            send_sem=send_sem.at[phase, k - 1],
            recv_sem=recv_sem.at[phase, k - 1],
            device_id={"tp": peer},
            device_id_type=MESH,
        )

    def gather(phase, k, owner):
        return pltpu.make_async_remote_copy(
            src_ref=full.at[phase, owner],
            dst_ref=full.at[phase, owner],
            send_sem=gsend_sem.at[phase, k - 1],
            recv_sem=grecv_sem.at[phase, k - 1],
            device_id={"tp": lax.rem(me + k, n)},
            device_id_type=MESH,
        )

    def handoff(b, k):
        return pltpu.make_async_remote_copy(
            src_ref=state_out.at[b, k - 1],
            dst_ref=state_in.at[b, k],
            send_sem=hsend_sem.at[b, k - 1],
            recv_sem=hrecv_sem.at[b, k - 1],
            device_id={"group": lax.rem(group + k, ng)},
            device_id_type=MESH,
        )

    for phase in range(2):
        if phase == 0:
            loads[0].wait()
            loads[1].wait()
            values = px[...]
        else:
            loads[2].wait()
            values = dx[...].reshape(steps * rows, channels)
        res = dot_nt(w[...], values)
        for j in range(n):
            part[phase, j] = res[j * piece:(j + 1) * piece]
        if phase == 0:
            pl.semaphore_wait(barrier, n - 1 + ng - 1)
            for k in range(1, n):
                scatter(phase, k).start()
            for i in (3, 4, 5, 6):
                loads[i].start()
    for i in range(7, 12):
        loads[i].wait()

    ends = []
    at = jnp.int32(0)
    for k in range(requests):
        at = at + len_ref[0, k]
        ends.append(at)
    leaving = []
    for k in range(ng):
        dest = lax.rem(group + k, ng)
        found = [jnp.int32(0)] * cap
        count = jnp.int32(0)
        for q in range(requests):
            hit = routes_ref[0, group * requests + q] == dest
            found = [jnp.where(hit & (count == r), jnp.maximum(ends[q] - 1, 0), found[r]) for r in range(cap)]
            count = count + hit.astype(jnp.int32)
        leaving.append(found)

    def locate(origin, carry):
        count, places = carry[0], list(carry[1:])
        arrived = jnp.int32(0)
        turn = lax.rem(group + ng - origin, ng)
        for q in range(requests):
            hit = routes_ref[0, origin * requests + q] == group
            places = [jnp.where(hit & (count == r), turn * cap + arrived, places[r]) for r in range(slots)]
            count = count + hit.astype(jnp.int32)
            arrived = arrived + hit.astype(jnp.int32)
        return (count, *places)

    located = lax.fori_loop(0, ng, locate, (jnp.int32(0),) * (slots + 1))
    taken, places = located[0], located[1:]

    def reduce(phase):
        total = part[phase, me]
        for k in range(1, n):
            scatter(phase, k).wait_recv()
            total = total + recv[phase, k - 1]
        full[phase, me] = total
        for k in range(1, n):
            gather(phase, k, me).start()

    reduce(0)
    for k in range(1, n):
        scatter(1, k).start()

    tile = (lax.broadcasted_iota(jnp.int32, (states, SET * states), 1) % states
            == lax.broadcasted_iota(jnp.int32, (states, SET * states), 0)).astype(BF16)

    def collect(phase):
        for k in range(1, n):
            gather(phase, k, lax.rem(me + n - k, n)).wait_recv()
        proj = jnp.concatenate([full[phase, j] for j in range(n)], axis=0)
        low[phase] = proj[:rank].astype(BF16)
        width = proj.shape[1]
        own = (lax.broadcasted_iota(jnp.int32, (SET * states, width), 0) // states
               == lax.broadcasted_iota(jnp.int32, (SET * states, width), 1) % SET)
        high, rest = [jnp.where(own, dot_tn(tile, v), 0.0).astype(BF16) for v in halves(proj[rank:rank + states])]
        for s in range(width // SET):
            lhs_b[phase, s] = jnp.concatenate([v[:, s * SET:(s + 1) * SET] for v in (high, rest, high)], axis=1)
        own = (lax.broadcasted_iota(jnp.int32, (width, SET * states), 1) // states
               == lax.broadcasted_iota(jnp.int32, (width, SET * states), 0) % SET)
        high, rest = [jnp.where(own, dot_tn(v, tile), 0.0).astype(BF16) for v in halves(proj[rank + states:])]
        for s in range(width // SET):
            lhs_c[phase, s, :SET] = high[s * SET:(s + 1) * SET]
            lhs_c[phase, s, SET:] = rest[s * SET:(s + 1) * SET]

    def forcing(phase, s, values):
        high, rest = halves(values)
        return jnp.dot(lhs_b[phase, s], jnp.concatenate([high, high, rest], axis=0), preferred_element_type=F32)

    def readout(phase, s, hidden):
        both = jnp.dot(lhs_c[phase, s], hidden.reshape(SET * states, block), preferred_element_type=F32)
        return both[:SET] + both[SET:]

    def step_sizes(phase, lanes):
        return softplus(dot_tn(low[phase], dtw[:, lanes]) + bias_ref[:, lanes])

    collect(0)
    loads[3].wait()
    loads[4].wait()
    position = lax.broadcasted_iota(jnp.int32, (tokens, block), 0)
    first = position == 0
    for k in range(requests - 1):
        first = first | (position == ends[k])

    def prefill_block(b, carry):
        lanes = pl.ds(pl.multiple_of(b * block, block), block)
        step = step_sizes(0, lanes)
        values = px[:, lanes].astype(F32)
        decay[...] = jnp.where(first, 1e30, step)
        pushes = step * values
        for s in range(tokens // SET):
            forced[s] = forcing(0, s, pushes[s * SET:(s + 1) * SET])
        rates = -jnp.exp(alog_ref[:, lanes]) * LOG2E

        def some(s, h):
            base = pl.multiple_of(s * SET, SET)
            for j in range(SET):
                da = jnp.exp2(decay[pl.ds(base + j, 1), :] * rates)
                h = da * h + forced[s, j * states:(j + 1) * states, :]
                hb[base + j] = h.astype(BF16)
            return h

        lax.fori_loop(0, tokens // SET, some, jnp.zeros((states, block), F32))
        for k in range(1, ng):
            for r in range(cap):
                state_out[b, k - 1, r] = hb[leaving[k][r]].astype(F32)
            handoff(b, k).start()
        for r in range(cap):
            state_in[b, 0, r] = hb[leaving[0][r]].astype(F32)
        mixed = jnp.concatenate([readout(0, s, hb[s * SET:(s + 1) * SET]) for s in range(tokens // SET)], axis=0)
        outp_ref[:, lanes] = ((mixed + skip_ref[:, lanes] * values) * silu(pg[:, lanes].astype(F32))).astype(BF16)
        return carry

    lax.fori_loop(0, blocks // 2, prefill_block, 0)
    reduce(1)
    lax.fori_loop(blocks // 2, blocks, prefill_block, 0)

    collect(1)
    loads[5].wait()
    loads[6].wait()

    def decode_rows(b, base, takes):
        lanes = pl.ds(pl.multiple_of(b * block, block), block)
        step = step_sizes(1, lanes).reshape(steps, rows, block)[:, base:base + SET]
        values = dx[:, base:base + SET, lanes].astype(F32)
        now = pl.ds(0, SET)
        for i in range(steps):
            decay[i * SET:(i + 1) * SET, :] = step[i]
            forced[i] = forcing(1, (i * rows + base) // SET, step[i] * values[i])
        rates = -jnp.exp(alog_ref[:, lanes]) * LOG2E
        if takes and base == 0:
            for k in range(1, ng):
                handoff(b, k).wait_recv()
            for k in range(ng):
                for r in range(cap):
                    pool[k * cap + r] = state_in[b, k, r]
        for j in range(SET):
            row = base + j
            h = cache[row, :, lanes]
            if takes and row < slots:
                place = places[row]
                h = jnp.where(row < taken, pool[place], h)
            for i in range(steps):
                da = jnp.exp2(decay[i * SET + j:i * SET + j + 1, :] * rates)
                h = da * h + forced[i, j * states:(j + 1) * states, :]
                hd[i, j] = h.astype(BF16)
        skip = skip_ref[:, lanes]
        for i in range(steps):
            mixed = readout(1, (i * rows + base) // SET, hd[i])
            gate = silu(dg[i, base:base + SET, lanes].astype(F32))
            outd_ref[i, base:base + SET, lanes] = ((mixed + skip * values[i]) * gate).astype(BF16)

    late = [base for base in range(0, rows, SET) if base < slots]
    early = [base for base in range(0, rows, SET) if base >= slots]

    def early_block(b, carry):
        for base in early:
            decode_rows(b, base, False)
        return carry

    def late_block(b, carry):
        for base in late:
            decode_rows(b, base, True)
        return carry

    lax.fori_loop(0, blocks, early_block, 0)
    lax.fori_loop(0, blocks, late_block, 0)

    for phase in range(2):
        for k in range(1, n):
            scatter(phase, k).wait_send()
            gather(phase, k, me).wait_send()

    def finish(b, carry):
        for k in range(1, ng):
            handoff(b, k).wait_send()
        return carry

    lax.fori_loop(0, blocks, finish, 0)


def local(n, ng, prefill_x, prefill_gate, lengths, routes, decode_x, decode_gate, cached_state,
          xproj_weight, dt_weight, dt_bias, a_log, skip_gain):
    tokens, channels = prefill_x.shape
    steps, rows, _ = decode_x.shape
    rank, states = dt_weight.shape[0], a_log.shape[0]
    width = xproj_weight.shape[1]
    cap = max(1, 2 * lengths.shape[1] // ng)
    block = min(512, channels)
    blocks = channels // block
    piece = width // n
    columns = max(tokens, steps * rows)
    anywhere = pl.BlockSpec(memory_space=pltpu.HBM)
    vmem = pl.BlockSpec(memory_space=pltpu.VMEM)
    dma = pltpu.SemaphoreType.DMA
    return pl.pallas_call(
        functools.partial(kernel, n, ng, cap, block),
        out_shape=(
            jax.ShapeDtypeStruct(prefill_x.shape, BF16),
            jax.ShapeDtypeStruct(decode_x.shape, BF16),
        ),
        in_specs=[anywhere] * 12,
        out_specs=(vmem, vmem),
        scratch_shapes=[
            pltpu.SMEM(lengths.shape, jnp.int32),
            pltpu.SMEM((1, routes.shape[0]), jnp.int32),
            pltpu.VMEM((1, channels), F32),
            pltpu.VMEM(a_log.shape, F32),
            pltpu.VMEM((1, channels), F32),
            pltpu.VMEM(prefill_x.shape, BF16),
            pltpu.VMEM(decode_x.shape, BF16),
            pltpu.VMEM((width, channels), BF16),
            pltpu.VMEM(prefill_x.shape, BF16),
            pltpu.VMEM(decode_x.shape, BF16),
            pltpu.VMEM(cached_state.shape, F32),
            pltpu.VMEM(dt_weight.shape, BF16),
            pltpu.VMEM((2, n, piece, columns), F32),
            pltpu.VMEM((2, n - 1, piece, columns), F32),
            pltpu.VMEM((2, n, piece, columns), F32),
            pltpu.VMEM((2, rank, columns), BF16),
            pltpu.VMEM((2, columns // SET, 2 * SET, SET * states), BF16),
            pltpu.VMEM((2, columns // SET, SET * states, 3 * SET), BF16),
            pltpu.VMEM((columns, block), F32),
            pltpu.VMEM((columns // SET, SET * states, block), F32),
            pltpu.VMEM((tokens, states, block), BF16),
            pltpu.VMEM((steps, SET, states, block), BF16),
            pltpu.VMEM((blocks, ng - 1, cap, states, block), F32),
            pltpu.VMEM((blocks, ng, cap, states, block), F32),
            pltpu.VMEM((ng * cap + lengths.shape[1], states, block), F32),
            dma((12,)),
            dma((2, n - 1)),
            dma((2, n - 1)),
            dma((2, n - 1)),
            dma((2, n - 1)),
            dma((blocks, ng - 1)),
            dma((blocks, ng - 1)),
        ],
        compiler_params=pltpu.CompilerParams(
            collective_id=0, has_side_effects=True, vmem_limit_bytes=60 * 1024 * 1024
        ),
        name="layer",
    )(lengths, routes.T, prefill_x, decode_x, xproj_weight.T, prefill_gate, decode_gate, cached_state, dt_weight,
      dt_bias[None], a_log, skip_gain[None])


def solution(mesh):
    placed = (
        P("group", "tp"),
        P("group", "tp"),
        P("group", None),
        P(),
        P(None, "group", "tp"),
        P(None, "group", "tp"),
        P("group", None, "tp"),
        P("tp", None),
        P(None, "tp"),
        P("tp"),
        P(None, "tp"),
        P("tp"),
    )
    return jax.shard_map(
        functools.partial(local, mesh.shape["tp"], mesh.shape["group"]),
        mesh=mesh,
        in_specs=placed,
        out_specs=(P("group", "tp"), P(None, "group", "tp")),
        check_vma=False,
    )
```

```python
import functools
import jax
import jax.numpy as jnp
from jax import lax
from jax.experimental import pallas as pl
from jax.experimental.pallas import tpu as pltpu
from jax.sharding import PartitionSpec as P

MESH = pl.DeviceIdType.MESH
F32 = jnp.float32
BF16 = jnp.bfloat16
LOG2E = 1.4426950408889634
SET = 16


def softplus(v):
    return jnp.maximum(v, 0.0) + jnp.log1p(jnp.exp(-jnp.abs(v)))


def silu(v):
    return v / (1.0 + jnp.exp(-v))


def dot_nt(a, b):
    return lax.dot_general(a, b, (((1,), (1,)), ((), ())), preferred_element_type=F32)


def dot_tn(a, b):
    return lax.dot_general(a, b, (((0,), (0,)), ((), ())), preferred_element_type=F32)


def halves(v):
    high = v.astype(BF16)
    return high, (v - high.astype(F32)).astype(BF16)


def kernel(n, ng, cap, block, len_hbm, routes_hbm, px_hbm, dx_hbm, w_hbm, pg_hbm, dg_hbm, cache_hbm, dtw_hbm,
           bias_hbm, alog_hbm, skip_hbm, outp_ref, outd_ref,
           len_ref, routes_ref, bias_ref, alog_ref, skip_ref,
           px, dx, w, pg, dg, cache, dtw, part, recv, full, low, lhs_c, lhs_b,
           decay, forced, hb, hd, state_out, state_in, pool,
           in_sem, send_sem, recv_sem, gsend_sem, grecv_sem, hsend_sem, hrecv_sem):
    me = lax.axis_index("tp")
    group = lax.axis_index("group")
    tokens, channels = px.shape
    steps, rows, _ = dx.shape
    rank = dtw.shape[0]
    states = alog_ref.shape[0]
    requests = len_ref.shape[1]
    blocks = channels // block
    piece = part.shape[2]
    slots = min(ng * cap, rows)

    loads = [
        pltpu.make_async_copy(src, dst, in_sem.at[i])
        for i, (src, dst) in enumerate(
            ((w_hbm, w), (px_hbm, px), (dx_hbm, dx), (dtw_hbm, dtw), (pg_hbm, pg), (cache_hbm, cache), (dg_hbm, dg),
             (len_hbm, len_ref), (routes_hbm, routes_ref), (bias_hbm, bias_ref), (alog_hbm, alog_ref),
             (skip_hbm, skip_ref))
        )
    ]
    for i in (0, 1, 2, 7, 8, 9, 10, 11):
        loads[i].start()
    barrier = pltpu.get_barrier_semaphore()
    for k in range(1, n):
        pl.semaphore_signal(barrier, inc=1, device_id={"tp": lax.rem(me + k, n)}, device_id_type=MESH)
    for k in range(1, ng):
        pl.semaphore_signal(barrier, inc=1, device_id={"group": lax.rem(group + k, ng)}, device_id_type=MESH)

    half = n // 2
    partner = me + 1 - 2 * lax.rem(me, 2)

    def even(j):
        return lax.rem(me + 2 * j, n)

    def to_partner(phase, j):
        return pltpu.make_async_remote_copy(
            src_ref=part.at[phase, lax.rem(partner + 2 * j, n)],
            dst_ref=recv.at[phase, j],
            send_sem=send_sem.at[phase, j],
            recv_sem=recv_sem.at[phase, j],
            device_id={"tp": partner},
            device_id_type=MESH,
        )

    def to_owner(phase, j):
        return pltpu.make_async_remote_copy(
            src_ref=part.at[phase, even(j)],
            dst_ref=recv.at[phase, half + j - 1],
            send_sem=send_sem.at[phase, half + j - 1],
            recv_sem=recv_sem.at[phase, half + j - 1],
            device_id={"tp": even(j)},
            device_id_type=MESH,
        )

    def pair_up(phase):
        for j in (*range(1, half), 0):
            to_partner(phase, j).start()

    def pass_on(phase):
        for j in range(1, half):
            to_partner(phase, j).wait_recv()
            part[phase, even(j)] = part[phase, even(j)] + recv[phase, j]
            to_owner(phase, j).start()

    def gather(phase, place, owner, device):
        return pltpu.make_async_remote_copy(
            src_ref=full.at[phase, owner],
            dst_ref=full.at[phase, owner],
            send_sem=gsend_sem.at[phase, place],
            recv_sem=grecv_sem.at[phase, place],
            device_id={"tp": device},
            device_id_type=MESH,
        )

    def handoff(b, k):
        return pltpu.make_async_remote_copy(
            src_ref=state_out.at[b, k - 1],
            dst_ref=state_in.at[b, k],
            send_sem=hsend_sem.at[b, k - 1],
            recv_sem=hrecv_sem.at[b, k - 1],
            device_id={"group": lax.rem(group + k, ng)},
            device_id_type=MESH,
        )

    for phase in range(2):
        if phase == 0:
            loads[0].wait()
            loads[1].wait()
            values = px[...]
        else:
            loads[2].wait()
            values = dx[...].reshape(steps * rows, channels)
        res = dot_nt(w[...], values)
        for j in range(n):
            part[phase, j] = res[j * piece:(j + 1) * piece]
        if phase == 0:
            pl.semaphore_wait(barrier, n - 1 + ng - 1)
            pair_up(0)
            for i in (3, 4, 5, 6):
                loads[i].start()
    pass_on(0)
    for i in range(7, 12):
        loads[i].wait()

    ends = []
    at = jnp.int32(0)
    for k in range(requests):
        at = at + len_ref[0, k]
        ends.append(at)
    leaving = []
    for k in range(ng):
        dest = lax.rem(group + k, ng)
        found = [jnp.int32(0)] * cap
        count = jnp.int32(0)
        for q in range(requests):
            hit = routes_ref[0, group * requests + q] == dest
            found = [jnp.where(hit & (count == r), jnp.maximum(ends[q] - 1, 0), found[r]) for r in range(cap)]
            count = count + hit.astype(jnp.int32)
        leaving.append(found)

    def locate(origin, carry):
        count, places = carry[0], list(carry[1:])
        arrived = jnp.int32(0)
        turn = lax.rem(group + ng - origin, ng)
        for q in range(requests):
            hit = routes_ref[0, origin * requests + q] == group
            places = [jnp.where(hit & (count == r), turn * cap + arrived, places[r]) for r in range(slots)]
            count = count + hit.astype(jnp.int32)
            arrived = arrived + hit.astype(jnp.int32)
        return (count, *places)

    located = lax.fori_loop(0, ng, locate, (jnp.int32(0),) * (slots + 1))
    taken, places = located[0], located[1:]

    def reduce(phase):
        to_partner(phase, 0).wait_recv()
        total = part[phase, me] + recv[phase, 0]
        for j in range(1, half):
            to_owner(phase, j).wait_recv()
            total = total + recv[phase, half + j - 1]
        full[phase, me] = total
        for j in range(1, half):
            gather(phase, 2 * j - 1, me, even(j)).start()
        gather(phase, 0, me, partner).start()

    reduce(0)
    pair_up(1)

    tile = (lax.broadcasted_iota(jnp.int32, (states, SET * states), 1) % states
            == lax.broadcasted_iota(jnp.int32, (states, SET * states), 0)).astype(BF16)

    def collect(phase):
        for j in range(1, half):
            source = lax.rem(me + n - 2 * j, n)
            gather(phase, 2 * j - 1, source, even(j)).wait_recv()
            gather(phase, 2 * j, source, partner).start()
        gather(phase, 0, partner, partner).wait_recv()
        for j in range(1, half):
            gather(phase, 2 * j, lax.rem(partner + n - 2 * j, n), partner).wait_recv()
        proj = jnp.concatenate([full[phase, j] for j in range(n)], axis=0)
        low[phase] = proj[:rank].astype(BF16)
        width = proj.shape[1]
        own = (lax.broadcasted_iota(jnp.int32, (SET * states, width), 0) // states
               == lax.broadcasted_iota(jnp.int32, (SET * states, width), 1) % SET)
        high, rest = [jnp.where(own, dot_tn(tile, v), 0.0).astype(BF16) for v in halves(proj[rank:rank + states])]
        for s in range(width // SET):
            lhs_b[phase, s] = jnp.concatenate([v[:, s * SET:(s + 1) * SET] for v in (high, rest, high)], axis=1)
        own = (lax.broadcasted_iota(jnp.int32, (width, SET * states), 1) // states
               == lax.broadcasted_iota(jnp.int32, (width, SET * states), 0) % SET)
        high, rest = [jnp.where(own, dot_tn(v, tile), 0.0).astype(BF16) for v in halves(proj[rank + states:])]
        for s in range(width // SET):
            lhs_c[phase, s, :SET] = high[s * SET:(s + 1) * SET]
            lhs_c[phase, s, SET:] = rest[s * SET:(s + 1) * SET]

    def forcing(phase, s, values):
        high, rest = halves(values)
        return jnp.dot(lhs_b[phase, s], jnp.concatenate([high, high, rest], axis=0), preferred_element_type=F32)

    def readout(phase, s, hidden):
        both = jnp.dot(lhs_c[phase, s], hidden.reshape(SET * states, block), preferred_element_type=F32)
        return both[:SET] + both[SET:]

    def step_sizes(phase, lanes):
        return softplus(dot_tn(low[phase], dtw[:, lanes]) + bias_ref[:, lanes])

    collect(0)
    pass_on(1)
    loads[3].wait()
    loads[4].wait()
    position = lax.broadcasted_iota(jnp.int32, (tokens, block), 0)
    first = position == 0
    for k in range(requests - 1):
        first = first | (position == ends[k])

    def prefill_block(b, carry):
        lanes = pl.ds(pl.multiple_of(b * block, block), block)
        step = step_sizes(0, lanes)
        values = px[:, lanes].astype(F32)
        decay[...] = jnp.where(first, 1e30, step)
        pushes = step * values
        for s in range(tokens // SET):
            forced[s] = forcing(0, s, pushes[s * SET:(s + 1) * SET])
        rates = -jnp.exp(alog_ref[:, lanes]) * LOG2E

        def some(s, h):
            base = pl.multiple_of(s * SET, SET)
            for j in range(SET):
                da = jnp.exp2(decay[pl.ds(base + j, 1), :] * rates)
                h = da * h + forced[s, j * states:(j + 1) * states, :]
                hb[base + j] = h.astype(BF16)
            return h

        lax.fori_loop(0, tokens // SET, some, jnp.zeros((states, block), F32))
        for k in range(1, ng):
            for r in range(cap):
                state_out[b, k - 1, r] = hb[leaving[k][r]].astype(F32)
            handoff(b, k).start()
        for r in range(cap):
            state_in[b, 0, r] = hb[leaving[0][r]].astype(F32)
        mixed = jnp.concatenate([readout(0, s, hb[s * SET:(s + 1) * SET]) for s in range(tokens // SET)], axis=0)
        outp_ref[:, lanes] = ((mixed + skip_ref[:, lanes] * values) * silu(pg[:, lanes].astype(F32))).astype(BF16)
        return carry

    lax.fori_loop(0, blocks // 2, prefill_block, 0)
    reduce(1)
    lax.fori_loop(blocks // 2, blocks, prefill_block, 0)

    collect(1)
    loads[5].wait()
    loads[6].wait()

    def decode_rows(b, base, takes):
        lanes = pl.ds(pl.multiple_of(b * block, block), block)
        step = step_sizes(1, lanes).reshape(steps, rows, block)[:, base:base + SET]
        values = dx[:, base:base + SET, lanes].astype(F32)
        now = pl.ds(0, SET)
        for i in range(steps):
            decay[i * SET:(i + 1) * SET, :] = step[i]
            forced[i] = forcing(1, (i * rows + base) // SET, step[i] * values[i])
        rates = -jnp.exp(alog_ref[:, lanes]) * LOG2E
        if takes and base == 0:
            for k in range(1, ng):
                handoff(b, k).wait_recv()
            for k in range(ng):
                for r in range(cap):
                    pool[k * cap + r] = state_in[b, k, r]
        for j in range(SET):
            row = base + j
            h = cache[row, :, lanes]
            if takes and row < slots:
                place = places[row]
                h = jnp.where(row < taken, pool[place], h)
            for i in range(steps):
                da = jnp.exp2(decay[i * SET + j:i * SET + j + 1, :] * rates)
                h = da * h + forced[i, j * states:(j + 1) * states, :]
                hd[i, j] = h.astype(BF16)
        skip = skip_ref[:, lanes]
        for i in range(steps):
            mixed = readout(1, (i * rows + base) // SET, hd[i])
            gate = silu(dg[i, base:base + SET, lanes].astype(F32))
            outd_ref[i, base:base + SET, lanes] = ((mixed + skip * values[i]) * gate).astype(BF16)

    late = [base for base in range(0, rows, SET) if base < slots]
    early = [base for base in range(0, rows, SET) if base >= slots]

    def early_block(b, carry):
        for base in early:
            decode_rows(b, base, False)
        return carry

    def late_block(b, carry):
        for base in late:
            decode_rows(b, base, True)
        return carry

    lax.fori_loop(0, blocks, early_block, 0)
    lax.fori_loop(0, blocks, late_block, 0)

    for phase in range(2):
        for j in range(half):
            to_partner(phase, j).wait_send()
        gather(phase, 0, me, partner).wait_send()
        for j in range(1, half):
            to_owner(phase, j).wait_send()
            gather(phase, 2 * j - 1, me, even(j)).wait_send()
            gather(phase, 2 * j, lax.rem(me + n - 2 * j, n), partner).wait_send()

    def finish(b, carry):
        for k in range(1, ng):
            handoff(b, k).wait_send()
        return carry

    lax.fori_loop(0, blocks, finish, 0)


def local(n, ng, prefill_x, prefill_gate, lengths, routes, decode_x, decode_gate, cached_state,
          xproj_weight, dt_weight, dt_bias, a_log, skip_gain):
    tokens, channels = prefill_x.shape
    steps, rows, _ = decode_x.shape
    rank, states = dt_weight.shape[0], a_log.shape[0]
    width = xproj_weight.shape[1]
    cap = max(1, 2 * lengths.shape[1] // ng)
    block = min(512, channels)
    blocks = channels // block
    piece = width // n
    columns = max(tokens, steps * rows)
    anywhere = pl.BlockSpec(memory_space=pltpu.HBM)
    vmem = pl.BlockSpec(memory_space=pltpu.VMEM)
    dma = pltpu.SemaphoreType.DMA
    return pl.pallas_call(
        functools.partial(kernel, n, ng, cap, block),
        out_shape=(
            jax.ShapeDtypeStruct(prefill_x.shape, BF16),
            jax.ShapeDtypeStruct(decode_x.shape, BF16),
        ),
        in_specs=[anywhere] * 12,
        out_specs=(vmem, vmem),
        scratch_shapes=[
            pltpu.SMEM(lengths.shape, jnp.int32),
            pltpu.SMEM((1, routes.shape[0]), jnp.int32),
            pltpu.VMEM((1, channels), F32),
            pltpu.VMEM(a_log.shape, F32),
            pltpu.VMEM((1, channels), F32),
            pltpu.VMEM(prefill_x.shape, BF16),
            pltpu.VMEM(decode_x.shape, BF16),
            pltpu.VMEM((width, channels), BF16),
            pltpu.VMEM(prefill_x.shape, BF16),
            pltpu.VMEM(decode_x.shape, BF16),
            pltpu.VMEM(cached_state.shape, F32),
            pltpu.VMEM(dt_weight.shape, BF16),
            pltpu.VMEM((2, n, piece, columns), F32),
            pltpu.VMEM((2, n - 1, piece, columns), F32),
            pltpu.VMEM((2, n, piece, columns), F32),
            pltpu.VMEM((2, rank, columns), BF16),
            pltpu.VMEM((2, columns // SET, 2 * SET, SET * states), BF16),
            pltpu.VMEM((2, columns // SET, SET * states, 3 * SET), BF16),
            pltpu.VMEM((columns, block), F32),
            pltpu.VMEM((columns // SET, SET * states, block), F32),
            pltpu.VMEM((tokens, states, block), BF16),
            pltpu.VMEM((steps, SET, states, block), BF16),
            pltpu.VMEM((blocks, ng - 1, cap, states, block), F32),
            pltpu.VMEM((blocks, ng, cap, states, block), F32),
            pltpu.VMEM((ng * cap + lengths.shape[1], states, block), F32),
            dma((12,)),
            dma((2, n - 1)),
            dma((2, n - 1)),
            dma((2, n - 1)),
            dma((2, n - 1)),
            dma((blocks, ng - 1)),
            dma((blocks, ng - 1)),
        ],
        compiler_params=pltpu.CompilerParams(
            collective_id=0, has_side_effects=True, vmem_limit_bytes=60 * 1024 * 1024
        ),
        name="layer",
    )(lengths, routes.T, prefill_x, decode_x, xproj_weight.T, prefill_gate, decode_gate, cached_state, dt_weight,
      dt_bias[None], a_log, skip_gain[None])


def solution(mesh):
    placed = (
        P("group", "tp"),
        P("group", "tp"),
        P("group", None),
        P(),
        P(None, "group", "tp"),
        P(None, "group", "tp"),
        P("group", None, "tp"),
        P("tp", None),
        P(None, "tp"),
        P("tp"),
        P(None, "tp"),
        P("tp"),
    )
    return jax.shard_map(
        functools.partial(local, mesh.shape["tp"], mesh.shape["group"]),
        mesh=mesh,
        in_specs=placed,
        out_specs=(P("group", "tp"), P(None, "group", "tp")),
        check_vma=False,
    )
```
